32 devices in a mesh: groups: 2 (over x), role: 8 (over z, y), head: 2 (over core).
Axes of the slice: x: 2, y: 2, z: 4, core: 2. Of those that a mesh axis runs over, the one named last changes fastest.
Arguments:
- queries: bfloat16 [128, 64, 576], P(('groups', 'role'), 'head'), parts along dimension 0, may hold values from -120 to 120
- kv_cache: bfloat16 [128, 256, 576], P(('groups', 'role')), parts along dimension 0, may hold values from -5 to 5
- cache_lengths: int32 [128], P(('groups', 'role')), parts along dimension 0, may hold values from 2 to 256, as said below
- uv_weight: bfloat16 [64, 512, 128], P('head'), may hold values from -0.25 to 0.25
- out_weight: bfloat16 [8192, 7168], P('head', 'role'), may hold values from -0.0625 to 0.0625
- residual: bfloat16 [128, 7168], P(('groups', 'role', 'head')), parts along dimension 0, may hold values from -6 to 6
- norm_gain: float32 [7168], replicated, may hold values from 0.25 to 1.75
- expert_ids: int32 [128, 2], P(('groups', 'role', 'head')), parts along dimension 0, may hold values from 0 to 7, all different within a row; in each aligned block of 4 rows (0 to 3, 4 to 7, ...) at most 2 rows name the same one
- route_weights: float32 [128, 2], P(('groups', 'role', 'head')), parts along dimension 0, may hold values from 0.25 to 1
- gate_weight: bfloat16 [7168, 16384], P(None, ('role', 'head')), may hold values from -0.0625 to 0.0625
- up_weight: bfloat16 [7168, 16384], P(None, ('role', 'head')), may hold values from -0.0625 to 0.0625
- down_weight: bfloat16 [16384, 7168], P(('role', 'head')), may hold values from -0.125 to 0.125
Outputs:
- layer_out: bfloat16 [128, 7168], P(('groups', 'role', 'head')), parts along dimension 0
The draws below stay inside these ranges and needn't reach their ends.
There are 2 independent parts, one for each index of `groups`. The reference program is written for one: setup_inputs(seed, part) draws one part's arguments, and reference() takes and returns one part's arrays. A program takes and returns all parts, laid end to end along the dimension named above; an argument that names none is the same for every part. Nothing has to cross between parts.
Inputs may be any that keep to these rules, and one draw needn't show every extreme that they name: `cache_lengths`: every request has at least 2 live positions and some request has 256. `expert_ids`: the 2 ids of a row differ; in each aligned block of 4 rows no id appears more than 2 times, and some id appears exactly 2 times in some block.
All inputs are finite; a program needn't handle non-finite values.
Results may differ from the reference program's by a relative error of at most 0.006.
Values may be sent and summed in bfloat16 or wider, within the bound.
No kernel may reach another device: no remote copies, remote signals or barrier semaphores. Data moves between devices by JAX's collectives and lax.ppermute only.
A program may use at most 128 MiB of HBM per device.

```python
import math
import jax
import jax.numpy as jnp
import numpy as np
from jax import lax

D = 7168
HEADS = 64
LATENT = 512
ROPE = 64
VDIM = 128
EFF = 2048
EXPERTS = 8
TOPK = 2
CTX = 256
TOKENS = 64
SHARE = 4
CAP = 2


def cache_base(key):
    return jnp.clip(jax.random.normal(key, (TOKENS, CTX, LATENT + ROPE), jnp.float32), -5.0, 5.0)


def draw_kv_cache(key, part):
    base = cache_base(key)
    return base.astype(jnp.bfloat16)


def draw_queries(key, part):
    key = jax.random.fold_in(key, 5)
    shape_full = (TOKENS, HEADS, LATENT + ROPE)
    values = jnp.clip(jax.random.normal(key, shape_full, jnp.float32), -5.0, 5.0)
    return values.astype(jnp.bfloat16)


def draw_cache_lengths(key, part):
    key = jax.random.fold_in(key, 3)
    lengths = jax.random.randint(key, (TOKENS,), 2, CTX + 1)
    return lengths.at[0].set(CTX).astype(jnp.int32)


def level_of(stream_key, extent, cuts, smallest, high):
    def one(dim, shards_of):
        draws = jax.random.uniform(jax.random.fold_in(jax.random.fold_in(stream_key, 6), dim), (shards_of,), jnp.float32, smallest / len(cuts), high / len(cuts))
        return jnp.repeat(jnp.exp(draws), extent[dim] // shards_of).reshape((-1,) + (1,) * (len(extent) - dim - 1))

    loudness = one(*cuts[0])
    for cut in cuts[1:]:
        loudness = loudness * one(*cut)
    return loudness


def routed_block(key, own, number, rows, count, top, limit, lean):
    ranking = jax.random.permutation(key, count)
    packed, common = shares(count, rows * top, limit, lean, True), shares(count, rows * top, limit, lean, False)
    places = jnp.arange(count)

    def named(tallies, offset_by):
        used = int((tallies > 0).sum())
        fixed = max(1, used // 4)
        shifted = fixed + (places - fixed + offset_by * (used - fixed)) % max(1, count - fixed)
        return jnp.zeros((count,), jnp.int32).at[ranking[jnp.where(places < fixed, places, shifted)]].set(jnp.asarray(tallies, jnp.int32))

    tallies = jnp.where(number % 4 == 0, named(packed, number // 4), named(common, number - number // 4 - 1))
    mixed = jax.random.permutation(jax.random.fold_in(own, 3), count)
    giver, receiver = mixed[0:count // 2 * 2:2], mixed[1:count // 2 * 2:2]
    slack = jnp.minimum(tallies[giver] - 1, limit - tallies[receiver]) // 2
    slack = jnp.where((giver == ranking[0]) | (receiver == ranking[0]) | (tallies[receiver] == 0), 0, jnp.maximum(slack, 0))
    shifted = jax.random.randint(jax.random.fold_in(own, 4), (count // 2,), 0, 1 << 20) % (slack + 1)
    tallies = tallies.at[giver].add(-shifted).at[receiver].add(shifted)
    members = jnp.searchsorted(jnp.cumsum(tallies), jnp.arange(rows * top), side="right").astype(jnp.int32)
    listing = members.reshape(top, rows).T
    listing = listing[jax.random.permutation(jax.random.fold_in(own, 1), rows)]
    offset_by = jax.random.randint(jax.random.fold_in(own, 2), (rows, 1), 0, top)
    return jnp.take_along_axis(listing, (jnp.arange(top)[None, :] + offset_by) % top, axis=1)


def shares(number_of, total, most, skew, full):
    portions = [(1 << 20) // math.isqrt(standing ** skew) + 1 for standing in range(1, number_of + 1)]
    largest = most if full else min(most, max(-(-total // number_of), total * portions[0] // sum(portions)))
    least = 1 if total - largest >= number_of - 1 else 0
    given, rest = [largest] + [least] * (number_of - 1), total - largest - least * (number_of - 1)
    while rest > 0:
        movable = [i for i in range(1, number_of) if given[i] < largest] or [i for i in range(1, number_of) if given[i] < most]
        pool, budget = sum([portions[i] for i in movable]), rest
        for i in movable:
            extra = min(most - given[i], max(1, budget * portions[i] // pool), rest)
            given[i] = given[i] + extra
            rest = rest - extra
    return np.array(given)


def noise(key, dims, scale, reach, cuts=(), held_as=jnp.bfloat16):
    gain = level_of(key, dims, cuts, -0.22, 0.18) if cuts else 1.0
    values = jax.random.normal(key, dims, jnp.float32) * scale * gain
    return jnp.minimum(jnp.maximum(values, -reach), reach).astype(held_as)


def setup_inputs(seed: int = 0, part: int = 0) -> dict:
    splits = jax.random.split(jax.random.key(seed), 13)
    own_keys = jax.random.split(jax.random.fold_in(splits[12], part), 13)
    queries = draw_queries(jax.random.fold_in(jax.random.fold_in(splits[12], part), 71), part)
    kv_cache = draw_kv_cache(jax.random.fold_in(jax.random.fold_in(splits[12], part), 71), part)
    cache_lengths = draw_cache_lengths(jax.random.fold_in(jax.random.fold_in(splits[12], part), 71), part)
    uv_weight = noise(splits[3], (HEADS, LATENT, VDIM), LATENT ** -0.5, 0.25, ((0, 2),))
    out_weight = noise(splits[4], (HEADS * VDIM, D), (HEADS * VDIM) ** -0.5, 0.0625, ((0, 2), (1, 8)))
    residual = noise(own_keys[5], (TOKENS, D), 1.0, 6.0, ((0, 16),))
    norm_gain = jnp.clip(1.0 + 0.15 * jax.random.normal(splits[6], (D,), jnp.float32), 0.25, 1.75)
    expert_ids_keys = jax.random.split(jax.random.fold_in(own_keys[7], 1), TOKENS // SHARE)
    expert_ids_turns = jax.random.permutation(jax.random.fold_in(own_keys[7], 3), TOKENS // SHARE)
    expert_ids = jax.vmap(lambda own, number: routed_block(jax.random.fold_in(own_keys[7], 2), own, number, SHARE, EXPERTS, TOPK, CAP, 2))(expert_ids_keys, expert_ids_turns).reshape((TOKENS, TOPK))
    route_weights = jnp.clip(0.25 + 0.75 * jax.random.uniform(own_keys[8], (TOKENS, TOPK), jnp.float32) ** level_of(own_keys[8], (TOKENS, TOPK), ((0, 16),), -0.2, 0.2), 0.25, 1.0)
    gate_weight = noise(splits[9], (D, EXPERTS * EFF), D ** -0.5, 0.0625, ((1, 16),))
    up_weight = noise(splits[10], (D, EXPERTS * EFF), D ** -0.5, 0.0625, ((1, 16),))
    down_weight = noise(splits[11], (EXPERTS * EFF, D), EFF ** -0.5, 0.125, ((0, 16),))
    return {"queries": queries, "kv_cache": kv_cache, "cache_lengths": cache_lengths, "uv_weight": uv_weight, "out_weight": out_weight, "residual": residual, "norm_gain": norm_gain, "expert_ids": expert_ids, "route_weights": route_weights, "gate_weight": gate_weight, "up_weight": up_weight, "down_weight": down_weight}


token_block = 64
assign_block = 32

def attend(args, uv_weight):
    query_rows, cache_rows, length_rows = args
    scale_factor = (VDIM + ROPE) ** (-0.5)
    scores = jnp.einsum('thc,tsc->ths', query_rows.astype(jnp.float32), cache_rows.astype(jnp.float32)) * scale_factor
    position = lax.broadcasted_iota(jnp.int32, scores.shape, 2)
    scores = jnp.where(position < length_rows[:, None, None], scores, -jnp.inf)
    top_score = lax.optimization_barrier(jnp.max(scores, axis=2, keepdims=True))
    weights = jnp.exp(scores - top_score)
    attn_probs = (weights / lax.optimization_barrier(jnp.sum(weights, axis=2, keepdims=True))).astype(jnp.bfloat16)
    latent_out = jnp.einsum('ths,tsc->thc', attn_probs.astype(jnp.float32), cache_rows[:, :, :LATENT].astype(jnp.float32)).astype(jnp.bfloat16)
    head_out = jnp.einsum('thc,hcv->thv', latent_out.astype(jnp.float32), uv_weight.astype(jnp.float32)).astype(jnp.bfloat16)
    return head_out.reshape(head_out.shape[0], HEADS * VDIM)

def reference(queries, kv_cache, cache_lengths, uv_weight, out_weight, residual, norm_gain, expert_ids, route_weights, gate_weight, up_weight, down_weight):
    blocks = TOKENS // token_block
    width_cols = LATENT + ROPE
    pieces = (queries.reshape(blocks, token_block, HEADS, width_cols), kv_cache.reshape(blocks, token_block, CTX, width_cols), cache_lengths.reshape(blocks, token_block))
    head_out = lax.map(lambda args: attend(args, uv_weight), pieces).reshape(TOKENS, HEADS * VDIM)
    attn_out = jnp.dot(head_out, out_weight, preferred_element_type=jnp.float32).astype(jnp.bfloat16)
    hidden = (residual.astype(jnp.float32) + attn_out.astype(jnp.float32)).astype(jnp.bfloat16)
    hidden_f = hidden.astype(jnp.float32)
    inverse = lax.rsqrt(lax.optimization_barrier(jnp.mean(hidden_f * hidden_f, axis=1, keepdims=True)) + 1e-06)
    normed = (hidden_f * inverse * norm_gain[None, :]).astype(jnp.bfloat16)
    flat_ids = expert_ids.reshape(-1).astype(jnp.int32)
    order = jnp.argsort(flat_ids, stable=True).astype(jnp.int32)
    sorted_ids = flat_ids[order]
    token_rows = normed[order // TOPK]
    count_blocks = TOKENS * TOPK // assign_block

    def run_block(block_id):
        ids_here = lax.dynamic_slice_in_dim(sorted_ids, block_id * assign_block, assign_block, 0)
        rows_here = lax.dynamic_slice_in_dim(token_rows, block_id * assign_block, assign_block, 0)

        def keep_going(carry):
            return carry[0] <= ids_here[assign_block - 1]

        def one_expert(carry):
            expert, accum = carry
            gate_cols = lax.dynamic_slice_in_dim(gate_weight, expert * EFF, EFF, 1)
            up_cols = lax.dynamic_slice_in_dim(up_weight, expert * EFF, EFF, 1)
            down_rows = lax.dynamic_slice_in_dim(down_weight, expert * EFF, EFF, 0)
            gate_val = jnp.dot(rows_here, gate_cols, preferred_element_type=jnp.float32)
            up_val = jnp.dot(rows_here, up_cols, preferred_element_type=jnp.float32)
            act_val = (jax.nn.silu(gate_val) * up_val).astype(jnp.bfloat16)
            result = jnp.dot(act_val, down_rows, preferred_element_type=jnp.float32)
            accum = accum + jnp.where((ids_here == expert)[:, None], result, jnp.zeros_like(result))
            return (expert + 1, accum)
        start_state = (ids_here[0], jnp.zeros((assign_block, D), jnp.float32))
        return lax.while_loop(keep_going, one_expert, start_state)[1]
    sorted_out = lax.map(run_block, jnp.arange(count_blocks, dtype=jnp.int32)).reshape(TOKENS * TOPK, D)
    expert_out = jnp.zeros_like(sorted_out).at[order].set(sorted_out)
    combined = lax.optimization_barrier(jnp.sum(route_weights[:, :, None] * expert_out.reshape(TOKENS, TOPK, D), axis=1))
    return (hidden_f + combined).astype(jnp.bfloat16)
```

```python
import functools

import jax
import jax.numpy as jnp
from jax import lax
from jax.experimental import pallas as pl
from jax.experimental.pallas import tpu as pltpu
from jax.sharding import PartitionSpec as P

LATENT = 512
ROPE = 64
VDIM = 128
EXPERTS = 8
CAP = 2
F32 = jnp.float32
BF16 = jnp.bfloat16
VMEM = pltpu.VMEM


def attend(queries, kv_cache, cache_lengths, uv_weight):
    scale_factor = (VDIM + ROPE) ** (-0.5)
    scores = (
        jnp.einsum("thc,tsc->ths", queries, kv_cache, preferred_element_type=jnp.float32)
        * scale_factor
    )
    position = lax.broadcasted_iota(jnp.int32, scores.shape, 2)
    scores = jnp.where(position < cache_lengths[:, None, None], scores, -jnp.inf)
    top_score = jnp.max(scores, axis=2, keepdims=True)
    weights = jnp.exp(scores - top_score)
    attn_probs = (weights / jnp.sum(weights, axis=2, keepdims=True)).astype(jnp.bfloat16)
    latent_out = jnp.einsum(
        "ths,tsc->thc", attn_probs, kv_cache[:, :, :LATENT], preferred_element_type=jnp.float32
    ).astype(jnp.bfloat16)
    head_out = jnp.einsum(
        "thc,hcv->thv", latent_out, uv_weight, preferred_element_type=jnp.float32
    ).astype(jnp.bfloat16)
    return head_out.reshape(head_out.shape[0], -1)


def slot_positions(expert_ids):
    flat_ids = expert_ids.reshape(-1)
    n = flat_ids.shape[0]
    earlier = lax.broadcasted_iota(jnp.int32, (n, n), 1) < lax.broadcasted_iota(
        jnp.int32, (n, n), 0
    )
    same = flat_ids[:, None] == flat_ids[None, :]
    rank = jnp.sum((earlier & same).astype(jnp.int32), axis=1)
    return (flat_ids * CAP + rank).reshape(expert_ids.shape)


def expert_kernel(mine_ref, other_ref, gate_ref, up_ref, down_ref, keep_ref, send_ref, x_ref, act_ref, *, wide, deep):
    half = mine_ref.shape[0]
    x_ref[:half, :] = mine_ref[...]
    x_ref[half:, :] = other_ref[...]

    def hidden_units(i, _):
        cols = pl.ds(pl.multiple_of(i * wide, wide), wide)
        gate = jnp.dot(x_ref[...], gate_ref[:, cols], preferred_element_type=F32)
        up = jnp.dot(x_ref[...], up_ref[:, cols], preferred_element_type=F32)
        act_ref[:, cols] = (gate / (1.0 + jnp.exp(-gate)) * up).astype(BF16)
        return 0

    lax.fori_loop(0, gate_ref.shape[1] // wide, hidden_units, 0)

    def model_columns(i, _):
        cols = pl.ds(pl.multiple_of(i * deep, deep), deep)
        part = jnp.dot(act_ref[...], down_ref[:, cols], preferred_element_type=F32)
        keep_ref[:, cols] = part[:half]
        send_ref[:, cols] = part[half:].astype(send_ref.dtype)
        return 0

    lax.fori_loop(0, down_ref.shape[1] // deep, model_columns, 0)


def run_experts(mine, other, gate, up, down):
    rows, width = mine.shape
    units = gate.shape[1]
    gate, up, down = [pltpu.with_memory_space_constraint(w, VMEM) for w in (gate, up, down)]
    whole = pl.BlockSpec(memory_space=VMEM)
    return pl.pallas_call(
        functools.partial(expert_kernel, wide=512, deep=1024),
        out_shape=(
            jax.ShapeDtypeStruct((rows, width), F32),
            jax.ShapeDtypeStruct((rows, width), F32),
        ),
        in_specs=[whole] * 5,
        out_specs=(whole, whole),
        scratch_shapes=[VMEM((2 * rows, width), BF16), VMEM((2 * rows, units), BF16)],
        compiler_params=pltpu.CompilerParams(vmem_limit_bytes=8 << 20),
        name="experts",
    )(mine, other, gate, up, down)


def fast(
    queries,
    kv_cache,
    cache_lengths,
    uv_weight,
    out_weight,
    residual,
    norm_gain,
    expert_ids,
    route_weights,
    gate_weight,
    up_weight,
    down_weight,
):
    roles = lax.axis_size("role")
    role = lax.axis_index("role")
    core = lax.axis_index("head")
    share = residual.shape[0]
    width = residual.shape[1]
    cols = width // roles
    tokens = 2 * share
    left = 4 * 128
    head_out = attend(queries, kv_cache, cache_lengths, uv_weight)
    positions = slot_positions(expert_ids)
    by_role = residual.reshape(share, roles, cols).transpose(1, 0, 2)
    note = jnp.pad(positions.astype(BF16), ((0, 0), (0, 126)))
    note = jnp.broadcast_to(note[None], (roles, share, 128))
    extra = jnp.concatenate(
        [by_role[:, :, :left], jnp.concatenate([by_role[:, :, left:], note], axis=2)], axis=1
    )
    messages = []
    for step in range(roles):
        block = jnp.concatenate(
            [head_out, lax.dynamic_index_in_dim(extra, role ^ step, 0, keepdims=False)], axis=1
        )
        if step:
            block = lax.ppermute(block, "role", [(i, i ^ step) for i in range(roles)])
        messages.append(block)
    gathered = jnp.concatenate(messages, axis=0)
    wide = head_out.shape[1]
    partial_value = jnp.dot(gathered[:, :wide], out_weight, preferred_element_type=F32)
    other_value = lax.ppermute(partial_value, "head", [(0, 1), (1, 0)])
    attn_out = (partial_value + other_value).astype(BF16)
    sides = gathered[:, wide:].reshape(roles, 2, share, left)
    resid = jnp.concatenate([sides[:, 0], sides[:, 1, :, : cols - left]], axis=2)
    own_pos = sides[:, 1, :, cols - left : cols - left + 2].astype(jnp.int32)
    own_attn = lax.dynamic_slice_in_dim(
        attn_out.reshape(roles, tokens, cols), core * share, share, 1
    )
    hidden = (resid.astype(F32) + own_attn.astype(F32)).astype(BF16).reshape(roles * share, cols)
    own_pos = own_pos.reshape(roles * share, 2)
    source = role ^ (lax.broadcasted_iota(jnp.int32, (1, 1, roles * share), 2) // share)
    dest = lax.broadcasted_iota(jnp.int32, (roles, 1, 1), 0)
    slot = lax.broadcasted_iota(jnp.int32, (1, roles * CAP, 1), 1)
    want = dest * CAP + slot % CAP
    placing = (slot // CAP == source) & (
        (own_pos[None, None, :, 0] == want) | (own_pos[None, None, :, 1] == want)
    )
    slots = jnp.einsum("djt,tc->djc", placing.astype(BF16), hidden, preferred_element_type=F32)
    slots = slots.astype(BF16)
    own = lax.broadcasted_iota(jnp.int32, (1, share, 1), 1)
    member = lax.broadcasted_iota(jnp.int32, (1, 1, roles * share), 2) % share
    keeping = ((source == dest) & (member == own)).astype(BF16)
    kept = jnp.einsum("dit,tc->dic", keeping, hidden, preferred_element_type=F32).astype(BF16)
    kept = jnp.pad(kept, ((0, 0), (0, 0), (0, 1024 - cols))).reshape(roles, share, 4, 256)
    kept = kept.transpose(0, 2, 1, 3).reshape(roles, 4 * share, 256)
    outgoing = jnp.concatenate([slots, kept], axis=2)
    received = lax.all_to_all(outgoing, "role", split_axis=0, concat_axis=0, tiled=True)
    x = received[:, :, :cols].transpose(1, 0, 2).reshape(roles * CAP, width).astype(F32)
    inverse = lax.rsqrt(jnp.mean(x * x, axis=1, keepdims=True) + 1e-06)
    normed = (x * inverse * norm_gain[None, :]).astype(BF16)
    hidden_own = (
        received[:, :, cols:]
        .reshape(roles, 4, share, 256)
        .transpose(2, 0, 1, 3)
        .reshape(share, roles, 1024)[:, :, :cols]
        .reshape(share, width)
    )
    other = lax.ppermute(normed, "head", [(0, 1), (1, 0)])
    keep, send = run_experts(normed, other, gate_weight, up_weight, down_weight)
    summed = (keep + lax.ppermute(send, "head", [(0, 1), (1, 0)])).astype(BF16)
    returned = lax.all_to_all(
        summed.reshape(roles, CAP, width), "role", split_axis=0, concat_axis=0, tiled=True
    )
    slot_grid = lax.broadcasted_iota(jnp.int32, (share, EXPERTS * CAP), 1)
    mixing = sum(
        jnp.where(slot_grid == positions[:, k : k + 1], route_weights[:, k : k + 1], 0.0)
        for k in range(2)
    )
    combined = jnp.dot(
        mixing,
        returned.reshape(EXPERTS * CAP, width).astype(F32),
        precision=lax.Precision.HIGHEST,
        preferred_element_type=F32,
    )
    return (hidden_own.astype(F32) + combined).astype(BF16)


def general(
    queries,
    kv_cache,
    cache_lengths,
    uv_weight,
    out_weight,
    residual,
    norm_gain,
    expert_ids,
    route_weights,
    gate_weight,
    up_weight,
    down_weight,
):
    role_n = lax.axis_size("role")
    head_n = lax.axis_size("head")
    share_rows = residual.shape[0]
    model_width = residual.shape[1]
    head_out = attend(queries, kv_cache, cache_lengths, uv_weight)
    partial_value = jnp.dot(
        lax.all_gather(head_out, "role", axis=0, tiled=True),
        out_weight,
        preferred_element_type=jnp.float32,
    )
    summed_cols = lax.psum(partial_value, "head").astype(jnp.bfloat16)
    own_rows = lax.all_to_all(summed_cols, "role", split_axis=0, concat_axis=1, tiled=True)
    attn_out = lax.dynamic_slice_in_dim(
        own_rows, lax.axis_index("head") * share_rows, share_rows, 0
    )
    hidden = (residual.astype(jnp.float32) + attn_out.astype(jnp.float32)).astype(jnp.bfloat16)
    hidden_f = hidden.astype(jnp.float32)
    inverse = lax.rsqrt(jnp.mean(hidden_f * hidden_f, axis=1, keepdims=True) + 1e-06)
    normed = (hidden_f * inverse * norm_gain[None, :]).astype(jnp.bfloat16)
    flat_ids = expert_ids.reshape(-1)
    onehot = (
        flat_ids[:, None] == lax.broadcasted_iota(jnp.int32, (flat_ids.shape[0], EXPERTS), 1)
    ).astype(jnp.int32)
    slot_rank = jnp.sum(onehot * (jnp.cumsum(onehot, axis=0) - onehot), axis=1).reshape(
        expert_ids.shape
    )
    position = expert_ids * CAP + slot_rank
    slot_grid = lax.broadcasted_iota(jnp.int32, (EXPERTS * CAP,) + expert_ids.shape, 0)
    matches = slot_grid == position[None, :, :]
    placing = jnp.any(matches, axis=2).astype(jnp.bfloat16)
    mixing = jnp.sum(jnp.where(matches, route_weights[None, :, :], 0.0), axis=2).T
    buffer = (
        jnp.dot(placing, normed, preferred_element_type=jnp.float32)
        .astype(jnp.bfloat16)
        .reshape(EXPERTS, CAP, model_width)
    )
    devices = role_n * head_n
    group_size = devices // EXPERTS
    outgoing = jnp.repeat(buffer, group_size, axis=0)
    received = lax.all_to_all(outgoing, ("role", "head"), split_axis=0, concat_axis=0, tiled=True)
    item_count = received.shape[1]
    token_rows = received.reshape(-1, model_width)
    gate_val = jnp.dot(token_rows, gate_weight, preferred_element_type=jnp.float32)
    up_val = jnp.dot(token_rows, up_weight, preferred_element_type=jnp.float32)
    act_val = (jax.nn.silu(gate_val) * up_val).astype(jnp.bfloat16)
    expert_part = jnp.dot(act_val, down_weight, preferred_element_type=jnp.float32).reshape(
        devices, item_count, model_width
    )
    returned = lax.all_to_all(
        expert_part, ("role", "head"), split_axis=0, concat_axis=0, tiled=True
    )
    expert_out = jnp.sum(returned.reshape(EXPERTS, group_size, CAP, model_width), axis=1)
    combined = jnp.dot(
        mixing,
        expert_out.reshape(EXPERTS * CAP, model_width),
        precision=lax.Precision.HIGHEST,
        preferred_element_type=jnp.float32,
    )
    return (hidden_f + combined).astype(jnp.bfloat16)


def on_device(*arrays):
    residual = arrays[5]
    roles = lax.axis_size("role")
    fits = roles == EXPERTS and lax.axis_size("head") == 2 and residual.shape[0] == 4
    return (fast if fits and residual.shape[1] == roles * 896 else general)(*arrays)


def solution(mesh):
    return jax.shard_map(
        on_device,
        mesh=mesh,
        in_specs=(
            P(("groups", "role"), "head", None),
            P(("groups", "role"), None, None),
            P(("groups", "role")),
            P("head", None, None),
            P("head", "role"),
            P(("groups", "role", "head"), None),
            P(),
            P(("groups", "role", "head"), None),
            P(("groups", "role", "head"), None),
            P(None, ("role", "head")),
            P(None, ("role", "head")),
            P(("role", "head"), None),
        ),
        out_specs=P(("groups", "role", "head"), None),
        check_vma=False,
    )
```

```python
import functools

import jax
import jax.numpy as jnp
from jax import lax
from jax.experimental import pallas as pl
from jax.experimental.pallas import tpu as pltpu
from jax.sharding import PartitionSpec as P

LATENT = 512
ROPE = 64
VDIM = 128
EXPERTS = 8
CAP = 2
F32 = jnp.float32
BF16 = jnp.bfloat16
VMEM = pltpu.VMEM


def attend(queries, kv_cache, cache_lengths, uv_weight):
    scale_factor = (VDIM + ROPE) ** (-0.5)
    scores = (
        jnp.einsum("thc,tsc->ths", queries, kv_cache, preferred_element_type=jnp.float32)
        * scale_factor
    )
    position = lax.broadcasted_iota(jnp.int32, scores.shape, 2)
    scores = jnp.where(position < cache_lengths[:, None, None], scores, -jnp.inf)
    top_score = jnp.max(scores, axis=2, keepdims=True)
    weights = jnp.exp(scores - top_score)
    attn_probs = (weights / jnp.sum(weights, axis=2, keepdims=True)).astype(jnp.bfloat16)
    latent_out = jnp.einsum(
        "ths,tsc->thc", attn_probs, kv_cache[:, :, :LATENT], preferred_element_type=jnp.float32
    ).astype(jnp.bfloat16)
    head_out = jnp.einsum(
        "thc,hcv->thv", latent_out, uv_weight, preferred_element_type=jnp.float32
    ).astype(jnp.bfloat16)
    return head_out.reshape(head_out.shape[0], -1)


def slot_positions(expert_ids):
    flat_ids = expert_ids.reshape(-1)
    n = flat_ids.shape[0]
    earlier = lax.broadcasted_iota(jnp.int32, (n, n), 1) < lax.broadcasted_iota(
        jnp.int32, (n, n), 0
    )
    same = flat_ids[:, None] == flat_ids[None, :]
    rank = jnp.sum((earlier & same).astype(jnp.int32), axis=1)
    return (flat_ids * CAP + rank).reshape(expert_ids.shape)


def load_kernel(gate_hbm, up_hbm, after_ref, both_ref, sems):
    copies = (
        pltpu.make_async_copy(gate_hbm, both_ref.at[0], sems.at[0]),
        pltpu.make_async_copy(up_hbm, both_ref.at[1], sems.at[1]),
    )
    for copy in copies:
        copy.start()
    for copy in copies:
        copy.wait()


def load(gate, up, after):
    gate, up = [pltpu.with_memory_space_constraint(w, pltpu.HBM) for w in (gate, up)]
    return pl.pallas_call(
        load_kernel,
        out_shape=VMEM((2,) + gate.shape, gate.dtype),
        in_specs=[pl.BlockSpec(memory_space=pltpu.HBM)] * 2 + [pl.BlockSpec(memory_space=pl.ANY)],
        out_specs=pl.BlockSpec(memory_space=VMEM),
        scratch_shapes=[pltpu.SemaphoreType.DMA((2,))],
        compiler_params=pltpu.CompilerParams(vmem_limit_bytes=1 << 20),
        cost_estimate=pl.CostEstimate(
            flops=0, bytes_accessed=2 * (gate.size + up.size), transcendentals=0
        ),
        name="load",
    )(gate, up, after)


def project_kernel(*refs):
    messages, (weight_hbm, out_ref, weight_ref, sems) = refs[:-4], refs[-4:]
    chunks, deep, _ = weight_ref.shape

    def fetch(i):
        return pltpu.make_async_copy(
            weight_hbm.at[pl.ds(i * deep, deep), :], weight_ref.at[i], sems.at[i]
        )

    for i in range(chunks):
        fetch(i).start()
    for i in range(chunks):
        rows = jnp.concatenate(
            [m[:, i * deep : (i + 1) * deep].astype(F32) for m in messages], axis=0
        ).astype(BF16)
        fetch(i).wait()
        part = jnp.dot(rows, weight_ref[i], preferred_element_type=F32)
        if i:
            out_ref[...] += part
        else:
            out_ref[...] = part


def project(messages, weight):
    depth, cols = weight.shape
    tokens = sum(m.shape[0] for m in messages)
    chunks = 4
    whole = pl.BlockSpec(memory_space=VMEM)
    return pl.pallas_call(
        project_kernel,
        out_shape=jax.ShapeDtypeStruct((tokens, cols), F32),
        in_specs=[whole] * len(messages) + [pl.BlockSpec(memory_space=pltpu.HBM)],
        out_specs=whole,
        scratch_shapes=[
            VMEM((chunks, depth // chunks, cols), BF16),
            pltpu.SemaphoreType.DMA((chunks,)),
        ],
        compiler_params=pltpu.CompilerParams(vmem_limit_bytes=12 << 20),
        cost_estimate=pl.CostEstimate(
            flops=2 * tokens * depth * cols, bytes_accessed=2 * depth * cols, transcendentals=0
        ),
        name="project",
    )(*messages, pltpu.with_memory_space_constraint(weight, pltpu.HBM))


def dispatch_kernel(place_ref, mine_ref, other_ref, *refs):
    messages, out_ref = refs[:-1], refs[-1]
    role, core = place_ref[0], place_ref[1]
    roles = len(messages)
    tokens, cols = mine_ref.shape
    each = tokens // roles
    share = each // 2
    wide = messages[0].shape[1]
    left = 4 * 128
    slots = roles * CAP
    firsts, seconds = [], []
    for m in messages:
        side = m[:, wide - left :].astype(F32)
        turned = pltpu.roll(side, share, 0)
        firsts.append(jnp.where(core == 0, side, turned))
        seconds.append(jnp.where(core == 0, turned, side))
    second = jnp.concatenate(seconds, axis=0)
    resid = jnp.concatenate([jnp.concatenate(firsts, axis=0), second[:, : cols - left]], axis=1)
    notes = second[:, cols - left :].T
    attn_out = (mine_ref[...] + other_ref[...]).astype(BF16)
    hidden = (resid + attn_out.astype(F32)).astype(BF16)
    token = lax.broadcasted_iota(jnp.int32, (1, tokens), 1)
    source = role ^ (token // each)
    member = token % each
    row = lax.broadcasted_iota(jnp.int32, (roles * slots, 1), 0)
    dest, slot = row // slots, row % slots
    want = (dest * CAP + slot % CAP).astype(F32)
    placing = (
        (slot // CAP == source)
        & (member // share == core)
        & ((notes[0:1, :] == want) | (notes[1:2, :] == want))
    )
    keeping = (dest == source) & (member == core * share + slot % share)
    placed = jnp.dot(
        jnp.where(placing, 1.0, 0.0).astype(BF16), hidden, preferred_element_type=F32
    ).astype(BF16)
    kept = jnp.dot(jnp.where(keeping, 1.0, 0.0).astype(BF16), hidden, preferred_element_type=F32)
    kept = jnp.concatenate([kept, jnp.zeros((roles * slots, 1024 - cols), F32)], axis=1)
    group = slot // share
    extra = kept[:, :256]
    for g in range(1, 4):
        extra = jnp.where(group == g, kept[:, g * 256 : (g + 1) * 256], extra)
    extra = extra.astype(BF16)
    for d in range(roles):
        out_ref[d, :, :cols] = placed[d * slots : (d + 1) * slots]
        out_ref[d, :, cols:] = extra[d * slots : (d + 1) * slots]


def dispatch(place, mine, other, messages):
    roles = len(messages)
    cols = mine.shape[1]
    whole = pl.BlockSpec(memory_space=VMEM)
    return pl.pallas_call(
        dispatch_kernel,
        out_shape=jax.ShapeDtypeStruct((roles, roles * CAP, cols + 256), BF16),
        in_specs=[pl.BlockSpec(memory_space=pltpu.SMEM)] + [whole] * (2 + roles),
        out_specs=whole,
        compiler_params=pltpu.CompilerParams(vmem_limit_bytes=6 << 20),
        name="dispatch",
    )(place, mine, other, *messages)


def expert_kernel(
    mine_ref, other_ref, both_ref, down_hbm, keep_ref, send_ref,
    x_ref, act_ref, down_ref, out_sems
):
    half, width = mine_ref.shape
    outs, _, broad = down_ref.shape

    def fetch_down(i):
        cols = pl.ds(i * broad, broad)
        return pltpu.make_async_copy(down_hbm.at[:, cols], down_ref.at[i], out_sems.at[i])

    for i in range(outs):
        fetch_down(i).start()
    x_ref[:half, :] = mine_ref[...]
    x_ref[half:, :] = other_ref[...]
    wide = 512

    def hidden_units(i, _):
        cols = pl.ds(pl.multiple_of(i * wide, wide), wide)
        gate = jnp.dot(x_ref[...], both_ref[0, :, cols], preferred_element_type=F32)
        up = jnp.dot(x_ref[...], both_ref[1, :, cols], preferred_element_type=F32)
        act_ref[:, cols] = (gate / (1.0 + jnp.exp(-gate)) * up).astype(BF16)
        return 0

    lax.fori_loop(0, both_ref.shape[2] // wide, hidden_units, 0)
    for i in range(outs):
        fetch_down(i).wait()
        part = jnp.dot(act_ref[...], down_ref[i], preferred_element_type=F32)
        keep_ref[:, i * broad : (i + 1) * broad] = part[:half]
        send_ref[:, i * broad : (i + 1) * broad] = part[half:].astype(send_ref.dtype)


def run_experts(mine, other, both, down):
    rows, width = mine.shape
    units = both.shape[2]
    outs = 7
    both = pltpu.with_memory_space_constraint(both, VMEM)
    down = pltpu.with_memory_space_constraint(down, pltpu.HBM)
    whole = pl.BlockSpec(memory_space=VMEM)
    return pl.pallas_call(
        expert_kernel,
        out_shape=(
            jax.ShapeDtypeStruct((rows, width), F32),
            jax.ShapeDtypeStruct((rows, width), F32),
        ),
        in_specs=[whole] * 3 + [pl.BlockSpec(memory_space=pltpu.HBM)],
        out_specs=(whole, whole),
        scratch_shapes=[
            VMEM((2 * rows, width), BF16),
            VMEM((2 * rows, units), BF16),
            VMEM((outs, units, width // outs), BF16),
            pltpu.SemaphoreType.DMA((outs,)),
        ],
        compiler_params=pltpu.CompilerParams(vmem_limit_bytes=18 << 20),
        cost_estimate=pl.CostEstimate(
            flops=12 * rows * width * units, bytes_accessed=2 * width * units, transcendentals=0
        ),
        name="experts",
    )(mine, other, both, down)


def fast(
    queries,
    kv_cache,
    cache_lengths,
    uv_weight,
    out_weight,
    residual,
    norm_gain,
    expert_ids,
    route_weights,
    gate_weight,
    up_weight,
    down_weight,
):
    roles = lax.axis_size("role")
    role = lax.axis_index("role")
    core = lax.axis_index("head")
    share = residual.shape[0]
    width = residual.shape[1]
    cols = width // roles
    tokens = 2 * share
    left = 4 * 128
    head_out = attend(queries, kv_cache, cache_lengths, uv_weight)
    place, head_out = lax.optimization_barrier((jnp.stack([role, core]), head_out))
    positions = slot_positions(expert_ids)
    by_role = residual.reshape(share, roles, cols).transpose(1, 0, 2)
    note = jnp.pad(positions.astype(BF16), ((0, 0), (0, 126)))
    note = jnp.broadcast_to(note[None], (roles, share, 128))
    extra = jnp.concatenate(
        [by_role[:, :, :left], jnp.concatenate([by_role[:, :, left:], note], axis=2)], axis=1
    )
    messages = []
    for step in range(roles):
        block = jnp.concatenate(
            [head_out, lax.dynamic_index_in_dim(extra, role ^ step, 0, keepdims=False)], axis=1
        )
        if step:
            block = lax.ppermute(block, "role", [(i, i ^ step) for i in range(roles)])
        messages.append(block)
    both_weights = load(gate_weight, up_weight, head_out)
    messages, both_weights = lax.optimization_barrier((messages, both_weights))
    partial_value = project(messages, out_weight)
    other_value = lax.ppermute(partial_value, "head", [(0, 1), (1, 0)])
    outgoing = dispatch(place, partial_value, other_value, messages)
    received = lax.all_to_all(outgoing, "role", split_axis=0, concat_axis=0, tiled=True)
    x = received[:, :, :cols].transpose(1, 0, 2).reshape(roles * CAP, width).astype(F32)
    inverse = lax.rsqrt(jnp.mean(x * x, axis=1, keepdims=True) + 1e-06)
    normed = (x * inverse * norm_gain[None, :]).astype(BF16)
    hidden_own = (
        received[:, :, cols:]
        .reshape(roles, 4, share, 256)
        .transpose(2, 0, 1, 3)
        .reshape(share, roles, 1024)[:, :, :cols]
        .reshape(share, width)
    )
    other = lax.ppermute(normed, "head", [(0, 1), (1, 0)])
    keep, send = run_experts(normed, other, both_weights, down_weight)
    summed = (keep + lax.ppermute(send, "head", [(0, 1), (1, 0)])).astype(BF16)
    returned = lax.all_to_all(
        summed.reshape(roles, CAP, width), "role", split_axis=0, concat_axis=0, tiled=True
    )
    slot_grid = lax.broadcasted_iota(jnp.int32, (share, EXPERTS * CAP), 1)
    mixing = sum(
        jnp.where(slot_grid == positions[:, k : k + 1], route_weights[:, k : k + 1], 0.0)
        for k in range(2)
    )
    combined = jnp.dot(
        mixing,
        returned.reshape(EXPERTS * CAP, width).astype(F32),
        precision=lax.Precision.HIGHEST,
        preferred_element_type=F32,
    )
    return (hidden_own.astype(F32) + combined).astype(BF16)


def general(
    queries,
    kv_cache,
    cache_lengths,
    uv_weight,
    out_weight,
    residual,
    norm_gain,
    expert_ids,
    route_weights,
    gate_weight,
    up_weight,
    down_weight,
):
    role_n = lax.axis_size("role")
    head_n = lax.axis_size("head")
    share_rows = residual.shape[0]
    model_width = residual.shape[1]
    head_out = attend(queries, kv_cache, cache_lengths, uv_weight)
    partial_value = jnp.dot(
        lax.all_gather(head_out, "role", axis=0, tiled=True),
        out_weight,
        preferred_element_type=jnp.float32,
    )
    summed_cols = lax.psum(partial_value, "head").astype(jnp.bfloat16)
    own_rows = lax.all_to_all(summed_cols, "role", split_axis=0, concat_axis=1, tiled=True)
    attn_out = lax.dynamic_slice_in_dim(
        own_rows, lax.axis_index("head") * share_rows, share_rows, 0
    )
    hidden = (residual.astype(jnp.float32) + attn_out.astype(jnp.float32)).astype(jnp.bfloat16)
    hidden_f = hidden.astype(jnp.float32)
    inverse = lax.rsqrt(jnp.mean(hidden_f * hidden_f, axis=1, keepdims=True) + 1e-06)
    normed = (hidden_f * inverse * norm_gain[None, :]).astype(jnp.bfloat16)
    flat_ids = expert_ids.reshape(-1)
    onehot = (
        flat_ids[:, None] == lax.broadcasted_iota(jnp.int32, (flat_ids.shape[0], EXPERTS), 1)
    ).astype(jnp.int32)
    slot_rank = jnp.sum(onehot * (jnp.cumsum(onehot, axis=0) - onehot), axis=1).reshape(
        expert_ids.shape
    )
    position = expert_ids * CAP + slot_rank
    slot_grid = lax.broadcasted_iota(jnp.int32, (EXPERTS * CAP,) + expert_ids.shape, 0)
    matches = slot_grid == position[None, :, :]
    placing = jnp.any(matches, axis=2).astype(jnp.bfloat16)
    mixing = jnp.sum(jnp.where(matches, route_weights[None, :, :], 0.0), axis=2).T
    buffer = (
        jnp.dot(placing, normed, preferred_element_type=jnp.float32)
        .astype(jnp.bfloat16)
        .reshape(EXPERTS, CAP, model_width)
    )
    devices = role_n * head_n
    group_size = devices // EXPERTS
    outgoing = jnp.repeat(buffer, group_size, axis=0)
    received = lax.all_to_all(outgoing, ("role", "head"), split_axis=0, concat_axis=0, tiled=True)
    item_count = received.shape[1]
    token_rows = received.reshape(-1, model_width)
    gate_val = jnp.dot(token_rows, gate_weight, preferred_element_type=jnp.float32)
    up_val = jnp.dot(token_rows, up_weight, preferred_element_type=jnp.float32)
    act_val = (jax.nn.silu(gate_val) * up_val).astype(jnp.bfloat16)
    expert_part = jnp.dot(act_val, down_weight, preferred_element_type=jnp.float32).reshape(
        devices, item_count, model_width
    )
    returned = lax.all_to_all(
        expert_part, ("role", "head"), split_axis=0, concat_axis=0, tiled=True
    )
    expert_out = jnp.sum(returned.reshape(EXPERTS, group_size, CAP, model_width), axis=1)
    combined = jnp.dot(
        mixing,
        expert_out.reshape(EXPERTS * CAP, model_width),
        precision=lax.Precision.HIGHEST,
        preferred_element_type=jnp.float32,
    )
    return (hidden_f + combined).astype(jnp.bfloat16)


def on_device(*arrays):
    residual = arrays[5]
    roles = lax.axis_size("role")
    fits = roles == EXPERTS and lax.axis_size("head") == 2 and residual.shape[0] == 4
    return (fast if fits and residual.shape[1] == roles * 896 else general)(*arrays)


def solution(mesh):
    return jax.shard_map(
        on_device,
        mesh=mesh,
        in_specs=(
            P(("groups", "role"), "head", None),
            P(("groups", "role"), None, None),
            P(("groups", "role")),
            P("head", None, None),
            P("head", "role"),
            P(("groups", "role", "head"), None),
            P(),
            P(("groups", "role", "head"), None),
            P(("groups", "role", "head"), None),
            P(None, ("role", "head")),
            P(None, ("role", "head")),
            P(("role", "head"), None),
        ),
        out_specs=P(("groups", "role", "head"), None),
        check_vma=False,
    )
```

```python
import functools

import jax
import jax.numpy as jnp
from jax import lax
from jax.experimental import pallas as pl
from jax.experimental.pallas import tpu as pltpu
from jax.sharding import PartitionSpec as P

LATENT = 512
ROPE = 64
VDIM = 128
EXPERTS = 8
CAP = 2
F32 = jnp.float32
BF16 = jnp.bfloat16
VMEM = pltpu.VMEM


def slot_of(ids_ref, token, choice):
    mine = ids_ref[choice, token]
    rank = jnp.int32(0)
    choices = ids_ref.shape[0]
    for earlier in range(token * choices + choice):
        rank += (ids_ref[earlier % choices, earlier // choices] == mine).astype(jnp.int32)
    return mine * CAP + rank


def attend_kernel(
    resid_ref, length_hbm, ids_hbm, query_hbm, cache_hbm, value_hbm, weight_hbm, weight_ref, *refs
):
    outs, refs = refs[:-11], refs[-11:]
    query_ref, cache_ref, value_ref, latent_ref, head_ref, side_ref, length_ref, ids_ref = refs[:8]
    cache_sems, value_sems, other_sems = refs[8:]
    requests, heads, _ = query_ref.shape
    groups = value_ref.shape[0]
    per = value_ref.shape[1]
    share, width = resid_ref.shape
    cols = width // len(outs)
    wide = heads * VDIM
    left = outs[0].shape[1] - wide
    role = lax.axis_index("role")
    scalars = [
        pltpu.make_async_copy(ids_hbm, ids_ref, other_sems.at[0]),
        pltpu.make_async_copy(length_hbm, length_ref, other_sems.at[1]),
    ]
    last = pltpu.make_async_copy(weight_hbm, weight_ref, other_sems.at[2])
    copies = [pltpu.make_async_copy(query_hbm, query_ref, other_sems.at[3])]
    for t in range(requests):
        copies.append(pltpu.make_async_copy(cache_hbm.at[t], cache_ref.at[t], cache_sems.at[t]))
    for g in range(groups):
        copies.append(
            pltpu.make_async_copy(
                value_hbm.at[pl.ds(g * per, per)], value_ref.at[g], value_sems.at[g]
            )
        )
    for copy in (*scalars, *copies, last):
        copy.start()
    for copy in scalars:
        copy.wait()

    side_ref[0:share, :width] = resid_ref[...].astype(F32)
    side_ref[share:, :width] = resid_ref[...].astype(F32)
    side_ref[:, width:] = jnp.zeros((2 * share, 128), F32)
    row = lax.broadcasted_iota(jnp.int32, (2 * share, 128), 0)
    lane = lax.broadcasted_iota(jnp.int32, (2 * share, 128), 1)
    notes = jnp.zeros((2 * share, 128), F32)
    for t in range(share):
        for k in range(2):
            slot = slot_of(ids_ref, t, k).astype(F32)
            notes = jnp.where((row == share + t) & (lane == k), slot, notes)
    upper = lax.broadcasted_iota(jnp.int32, (2 * share, left), 0) < share
    for step, out in enumerate(outs):
        start = pl.multiple_of((role ^ step) * cols, 128)
        first = side_ref[:, pl.ds(start, left)]
        second = side_ref[:, pl.ds(start + left, cols - left)]
        second = jnp.concatenate([second, notes], axis=1)
        out[:, wide:] = jnp.where(upper, first, second).astype(BF16)

    scale = (VDIM + ROPE) ** (-0.5)
    for copy in copies[: 1 + requests]:
        copy.wait()
    scores = [
        jnp.dot(query_ref[t], cache_ref[t], preferred_element_type=F32) for t in range(requests)
    ]
    position = lax.broadcasted_iota(jnp.int32, scores[0].shape, 1)
    scores = [
        jnp.where(position < length_ref[t], scores[t] * scale, -jnp.inf) for t in range(requests)
    ]
    tops = [jnp.max(v, axis=1, keepdims=True) for v in scores]
    weights = [jnp.exp(v - top) for v, top in zip(scores, tops)]
    sums = [jnp.sum(v, axis=1, keepdims=True) for v in weights]
    probs = [(v / total).astype(BF16) for v, total in zip(weights, sums)]
    for t in range(requests):
        latent = lax.dot_general(
            probs[t], cache_ref[t, :LATENT], (((1,), (1,)), ((), ())), preferred_element_type=F32
        )
        latent = latent.astype(BF16).astype(F32)
        for c in range(LATENT // 128):
            latent_ref[c, t * heads : (t + 1) * heads, :] = latent[:, c * 128 : (c + 1) * 128]
    for copy in copies[1 + requests :]:
        copy.wait()
    for g in range(groups):
        for i in range(per):
            h = g * per + i
            latent = jnp.concatenate(
                [
                    latent_ref[c, pl.ds(h, requests, stride=heads), :]
                    for c in range(LATENT // 128)
                ],
                axis=1,
            ).astype(BF16)
            head = jnp.dot(latent, value_ref[g, i], preferred_element_type=F32)
            head_ref[:, h * VDIM : (h + 1) * VDIM] = head.astype(BF16)
    for out in outs:
        out[:, :wide] = head_ref[...]
    last.wait()


def attend(lengths, ids, residual, queries, cache, values, weight, roles):
    requests, heads, width = queries.shape
    groups = 4
    hbm = [
        pltpu.with_memory_space_constraint(w, pltpu.HBM)
        for w in (lengths, ids, queries, cache, values, weight)
    ]
    whole = pl.BlockSpec(memory_space=VMEM)
    return pl.pallas_call(
        attend_kernel,
        out_shape=(VMEM(weight.shape, weight.dtype),)
        + (jax.ShapeDtypeStruct((requests, heads * VDIM + 512), BF16),) * roles,
        in_specs=[whole] + [pl.BlockSpec(memory_space=pltpu.HBM)] * 6,
        out_specs=(whole,) * (1 + roles),
        scratch_shapes=[
            VMEM(queries.shape, BF16),
            VMEM(cache.shape, BF16),
            VMEM((groups, heads // groups) + values.shape[1:], BF16),
            VMEM((LATENT // 128, requests * heads, 128), F32),
            VMEM((requests, heads * VDIM), BF16),
            VMEM((2 * residual.shape[0], residual.shape[1] + 128), F32),
            pltpu.SMEM(lengths.shape, jnp.int32),
            pltpu.SMEM(ids.shape, jnp.int32),
            pltpu.SemaphoreType.DMA((requests,)),
            pltpu.SemaphoreType.DMA((groups,)),
            pltpu.SemaphoreType.DMA((4,)),
        ],
        compiler_params=pltpu.CompilerParams(vmem_limit_bytes=24 << 20),
        name="attend",
    )(residual, *hbm)


def combine_kernel(ids_ref, route_ref, received_ref, returned_ref, out_ref, sum_ref):
    roles, slots, _ = received_ref.shape
    share, width = out_ref.shape
    cols = width // roles
    for r in range(roles):
        kept = received_ref[r, :, cols:].astype(F32)
        for g in range(4):
            reach = min(256, cols - g * 256)
            start = r * cols + g * 256
            sum_ref[:, start : start + reach] = kept[g * share : (g + 1) * share, :reach]
    for t in range(share):
        extra = []
        for k in range(2):
            slot = slot_of(ids_ref, t, k)
            both = returned_ref[ids_ref[k, t]].astype(F32)
            one = jnp.where(slot % CAP == 0, both[0:1], both[1:2])
            extra.append(route_ref[k, t] * one)
        sum_ref[t : t + 1, :] += extra[0] + extra[1]
    out_ref[...] = sum_ref[...].astype(BF16)


def combine(ids, route, received, returned, share):
    width = returned.shape[2]
    whole = pl.BlockSpec(memory_space=VMEM)
    scalars = pl.BlockSpec(memory_space=pltpu.SMEM)
    return pl.pallas_call(
        combine_kernel,
        out_shape=jax.ShapeDtypeStruct((share, width), BF16),
        in_specs=[scalars] * 2 + [whole] * 2,
        out_specs=whole,
        scratch_shapes=[VMEM((share, width), F32)],
        compiler_params=pltpu.CompilerParams(vmem_limit_bytes=6 << 20),
        name="combine",
    )(ids, route, received, returned)


def load_kernel(gate_hbm, up_hbm, after_ref, both_ref, sems):
    copies = (
        pltpu.make_async_copy(gate_hbm, both_ref.at[0], sems.at[0]),
        pltpu.make_async_copy(up_hbm, both_ref.at[1], sems.at[1]),
    )
    for copy in copies:
        copy.start()
    for copy in copies:
        copy.wait()


def load(gate, up, after):
    gate, up = [pltpu.with_memory_space_constraint(w, pltpu.HBM) for w in (gate, up)]
    return pl.pallas_call(
        load_kernel,
        out_shape=VMEM((2,) + gate.shape, gate.dtype),
        in_specs=[pl.BlockSpec(memory_space=pltpu.HBM)] * 2 + [pl.BlockSpec(memory_space=pl.ANY)],
        out_specs=pl.BlockSpec(memory_space=VMEM),
        scratch_shapes=[pltpu.SemaphoreType.DMA((2,))],
        compiler_params=pltpu.CompilerParams(vmem_limit_bytes=1 << 20),
        cost_estimate=pl.CostEstimate(
            flops=0, bytes_accessed=2 * (gate.size + up.size), transcendentals=0
        ),
        name="load",
    )(gate, up, after)


def project_kernel(weight_ref, *refs):
    messages, out_ref = refs[:-1], refs[-1]
    depth = weight_ref.shape[0]
    rows = jnp.concatenate([m[:, :depth].astype(F32) for m in messages], axis=0).astype(BF16)
    out_ref[...] = jnp.dot(rows, weight_ref[...], preferred_element_type=F32)


def project(messages, weight):
    cols = weight.shape[1]
    tokens = sum(m.shape[0] for m in messages)
    whole = pl.BlockSpec(memory_space=VMEM)
    return pl.pallas_call(
        project_kernel,
        out_shape=jax.ShapeDtypeStruct((tokens, cols), F32),
        in_specs=[whole] * (1 + len(messages)),
        out_specs=whole,
        compiler_params=pltpu.CompilerParams(vmem_limit_bytes=6 << 20),
        name="project",
    )(pltpu.with_memory_space_constraint(weight, VMEM), *messages)


def dispatch_kernel(mine_ref, other_ref, *refs):
    messages, out_ref = refs[:-1], refs[-1]
    role, core = lax.axis_index("role"), lax.axis_index("head")
    roles = len(messages)
    tokens, cols = mine_ref.shape
    each = tokens // roles
    share = each // 2
    wide = messages[0].shape[1]
    left = 4 * 128
    slots = roles * CAP
    firsts, seconds = [], []
    for m in messages:
        side = m[:, wide - left :].astype(F32)
        turned = pltpu.roll(side, share, 0)
        firsts.append(jnp.where(core == 0, side, turned))
        seconds.append(jnp.where(core == 0, turned, side))
    second = jnp.concatenate(seconds, axis=0)
    resid = jnp.concatenate([jnp.concatenate(firsts, axis=0), second[:, : cols - left]], axis=1)
    notes = second[:, cols - left :].T
    attn_out = (mine_ref[...] + other_ref[...]).astype(BF16)
    hidden = (resid + attn_out.astype(F32)).astype(BF16)
    token = lax.broadcasted_iota(jnp.int32, (1, tokens), 1)
    source = role ^ (token // each)
    member = token % each
    row = lax.broadcasted_iota(jnp.int32, (roles * slots, 1), 0)
    dest, slot = row // slots, row % slots
    want = (dest * CAP + slot % CAP).astype(F32)
    placing = (
        (slot // CAP == source)
        & (member // share == core)
        & ((notes[0:1, :] == want) | (notes[1:2, :] == want))
    )
    keeping = (dest == source) & (member == core * share + slot % share)
    placed = jnp.dot(
        jnp.where(placing, 1.0, 0.0).astype(BF16), hidden, preferred_element_type=F32
    ).astype(BF16)
    kept = jnp.dot(jnp.where(keeping, 1.0, 0.0).astype(BF16), hidden, preferred_element_type=F32)
    kept = jnp.concatenate([kept, jnp.zeros((roles * slots, 1024 - cols), F32)], axis=1)
    group = slot // share
    extra = kept[:, :256]
    for g in range(1, 4):
        extra = jnp.where(group == g, kept[:, g * 256 : (g + 1) * 256], extra)
    extra = extra.astype(BF16)
    for d in range(roles):
        out_ref[d, :, :cols] = placed[d * slots : (d + 1) * slots]
        out_ref[d, :, cols:] = extra[d * slots : (d + 1) * slots]


def dispatch(mine, other, messages):
    roles = len(messages)
    cols = mine.shape[1]
    whole = pl.BlockSpec(memory_space=VMEM)
    return pl.pallas_call(
        dispatch_kernel,
        out_shape=jax.ShapeDtypeStruct((roles, roles * CAP, cols + 256), BF16),
        in_specs=[whole] * (2 + roles),
        out_specs=whole,
        compiler_params=pltpu.CompilerParams(vmem_limit_bytes=6 << 20),
        name="dispatch",
    )(mine, other, *messages)


def expert_kernel(
    mine_ref, other_ref, both_ref, down_hbm, keep_ref, send_ref,
    x_ref, act_ref, down_ref, out_sems
):
    half, width = mine_ref.shape
    outs, _, broad = down_ref.shape

    def fetch_down(i):
        cols = pl.ds(i * broad, broad)
        return pltpu.make_async_copy(down_hbm.at[:, cols], down_ref.at[i], out_sems.at[i])

    for i in range(outs):
        fetch_down(i).start()
    x_ref[:half, :] = mine_ref[...]
    x_ref[half:, :] = other_ref[...]
    wide = 512

    def hidden_units(i, _):
        cols = pl.ds(pl.multiple_of(i * wide, wide), wide)
        gate = jnp.dot(x_ref[...], both_ref[0, :, cols], preferred_element_type=F32)
        up = jnp.dot(x_ref[...], both_ref[1, :, cols], preferred_element_type=F32)
        act_ref[:, cols] = (gate / (1.0 + jnp.exp(-gate)) * up).astype(BF16)
        return 0

    lax.fori_loop(0, both_ref.shape[2] // wide, hidden_units, 0)
    for i in range(outs):
        fetch_down(i).wait()
        part = jnp.dot(act_ref[...], down_ref[i], preferred_element_type=F32)
        keep_ref[:, i * broad : (i + 1) * broad] = part[:half]
        send_ref[:, i * broad : (i + 1) * broad] = part[half:].astype(send_ref.dtype)


def run_experts(mine, other, both, down):
    rows, width = mine.shape
    units = both.shape[2]
    outs = 7
    both = pltpu.with_memory_space_constraint(both, VMEM)
    down = pltpu.with_memory_space_constraint(down, pltpu.HBM)
    whole = pl.BlockSpec(memory_space=VMEM)
    return pl.pallas_call(
        expert_kernel,
        out_shape=(
            jax.ShapeDtypeStruct((rows, width), F32),
            jax.ShapeDtypeStruct((rows, width), F32),
        ),
        in_specs=[whole] * 3 + [pl.BlockSpec(memory_space=pltpu.HBM)],
        out_specs=(whole, whole),
        scratch_shapes=[
            VMEM((2 * rows, width), BF16),
            VMEM((2 * rows, units), BF16),
            VMEM((outs, units, width // outs), BF16),
            pltpu.SemaphoreType.DMA((outs,)),
        ],
        compiler_params=pltpu.CompilerParams(vmem_limit_bytes=18 << 20),
        cost_estimate=pl.CostEstimate(
            flops=12 * rows * width * units, bytes_accessed=2 * width * units, transcendentals=0
        ),
        name="experts",
    )(mine, other, both, down)


def fast(
    queries,
    kv_cache,
    cache_lengths,
    uv_weight,
    out_weight,
    residual,
    norm_gain,
    expert_ids,
    route_weights,
    gate_weight,
    up_weight,
    down_weight,
):
    roles = lax.axis_size("role")
    share = residual.shape[0]
    width = residual.shape[1]
    cols = width // roles
    ids = expert_ids.T
    cache = kv_cache.transpose(0, 2, 1)
    out_weight, *messages = attend(
        cache_lengths, ids, residual, queries, cache, uv_weight, out_weight, roles
    )
    both_weights = load(gate_weight, up_weight, messages[0])
    messages = [messages[0]] + [
        lax.ppermute(messages[step], "role", [(i, i ^ step) for i in range(roles)])
        for step in range(1, roles)
    ]
    messages, both_weights = lax.optimization_barrier((messages, both_weights))
    partial_value = project(messages, out_weight)
    other_value = lax.ppermute(partial_value, "head", [(0, 1), (1, 0)])
    outgoing = dispatch(partial_value, other_value, messages)
    received = lax.all_to_all(outgoing, "role", split_axis=0, concat_axis=0, tiled=True)
    x = received[:, :, :cols].transpose(1, 0, 2).reshape(roles * CAP, width).astype(F32)
    inverse = lax.rsqrt(jnp.mean(x * x, axis=1, keepdims=True) + 1e-06)
    normed = (x * inverse * norm_gain[None, :]).astype(BF16)
    other = lax.ppermute(normed, "head", [(0, 1), (1, 0)])
    keep, send = run_experts(normed, other, both_weights, down_weight)
    summed = (keep + lax.ppermute(send, "head", [(0, 1), (1, 0)])).astype(BF16)
    returned = lax.all_to_all(
        summed.reshape(roles, CAP, width), "role", split_axis=0, concat_axis=0, tiled=True
    )
    return combine(ids, route_weights.T, received, returned, share)


def attend_general(queries, kv_cache, cache_lengths, uv_weight):
    scale_factor = (VDIM + ROPE) ** (-0.5)
    scores = (
        jnp.einsum("thc,tsc->ths", queries, kv_cache, preferred_element_type=jnp.float32)
        * scale_factor
    )
    position = lax.broadcasted_iota(jnp.int32, scores.shape, 2)
    scores = jnp.where(position < cache_lengths[:, None, None], scores, -jnp.inf)
    top_score = jnp.max(scores, axis=2, keepdims=True)
    weights = jnp.exp(scores - top_score)
    attn_probs = (weights / jnp.sum(weights, axis=2, keepdims=True)).astype(jnp.bfloat16)
    latent_out = jnp.einsum(
        "ths,tsc->thc", attn_probs, kv_cache[:, :, :LATENT], preferred_element_type=jnp.float32
    ).astype(jnp.bfloat16)
    head_out = jnp.einsum(
        "thc,hcv->thv", latent_out, uv_weight, preferred_element_type=jnp.float32
    ).astype(jnp.bfloat16)
    return head_out.reshape(head_out.shape[0], -1)


def general(
    queries,
    kv_cache,
    cache_lengths,
    uv_weight,
    out_weight,
    residual,
    norm_gain,
    expert_ids,
    route_weights,
    gate_weight,
    up_weight,
    down_weight,
):
    role_n = lax.axis_size("role")
    head_n = lax.axis_size("head")
    share_rows = residual.shape[0]
    model_width = residual.shape[1]
    head_out = attend_general(queries, kv_cache, cache_lengths, uv_weight)
    partial_value = jnp.dot(
        lax.all_gather(head_out, "role", axis=0, tiled=True),
        out_weight,
        preferred_element_type=jnp.float32,
    )
    summed_cols = lax.psum(partial_value, "head").astype(jnp.bfloat16)
    own_rows = lax.all_to_all(summed_cols, "role", split_axis=0, concat_axis=1, tiled=True)
    attn_out = lax.dynamic_slice_in_dim(
        own_rows, lax.axis_index("head") * share_rows, share_rows, 0
    )
    hidden = (residual.astype(jnp.float32) + attn_out.astype(jnp.float32)).astype(jnp.bfloat16)
    hidden_f = hidden.astype(jnp.float32)
    inverse = lax.rsqrt(jnp.mean(hidden_f * hidden_f, axis=1, keepdims=True) + 1e-06)
    normed = (hidden_f * inverse * norm_gain[None, :]).astype(jnp.bfloat16)
    flat_ids = expert_ids.reshape(-1)
    onehot = (
        flat_ids[:, None] == lax.broadcasted_iota(jnp.int32, (flat_ids.shape[0], EXPERTS), 1)
    ).astype(jnp.int32)
    slot_rank = jnp.sum(onehot * (jnp.cumsum(onehot, axis=0) - onehot), axis=1).reshape(
        expert_ids.shape
    )
    position = expert_ids * CAP + slot_rank
    slot_grid = lax.broadcasted_iota(jnp.int32, (EXPERTS * CAP,) + expert_ids.shape, 0)
    matches = slot_grid == position[None, :, :]
    placing = jnp.any(matches, axis=2).astype(jnp.bfloat16)
    mixing = jnp.sum(jnp.where(matches, route_weights[None, :, :], 0.0), axis=2).T
    buffer = (
        jnp.dot(placing, normed, preferred_element_type=jnp.float32)
        .astype(jnp.bfloat16)
        .reshape(EXPERTS, CAP, model_width)
    )
    devices = role_n * head_n
    group_size = devices // EXPERTS
    outgoing = jnp.repeat(buffer, group_size, axis=0)
    received = lax.all_to_all(outgoing, ("role", "head"), split_axis=0, concat_axis=0, tiled=True)
    item_count = received.shape[1]
    token_rows = received.reshape(-1, model_width)
    gate_val = jnp.dot(token_rows, gate_weight, preferred_element_type=jnp.float32)
    up_val = jnp.dot(token_rows, up_weight, preferred_element_type=jnp.float32)
    act_val = (jax.nn.silu(gate_val) * up_val).astype(jnp.bfloat16)
    expert_part = jnp.dot(act_val, down_weight, preferred_element_type=jnp.float32).reshape(
        devices, item_count, model_width
    )
    returned = lax.all_to_all(
        expert_part, ("role", "head"), split_axis=0, concat_axis=0, tiled=True
    )
    expert_out = jnp.sum(returned.reshape(EXPERTS, group_size, CAP, model_width), axis=1)
    combined = jnp.dot(
        mixing,
        expert_out.reshape(EXPERTS * CAP, model_width),
        precision=lax.Precision.HIGHEST,
        preferred_element_type=jnp.float32,
    )
    return (hidden_f + combined).astype(jnp.bfloat16)


def on_device(*arrays):
    residual = arrays[5]
    roles = lax.axis_size("role")
    fits = roles == EXPERTS and lax.axis_size("head") == 2 and residual.shape[0] == 4
    return (fast if fits and residual.shape[1] == roles * 896 else general)(*arrays)


def solution(mesh):
    return jax.shard_map(
        on_device,
        mesh=mesh,
        in_specs=(
            P(("groups", "role"), "head", None),
            P(("groups", "role"), None, None),
            P(("groups", "role")),
            P("head", None, None),
            P("head", "role"),
            P(("groups", "role", "head"), None),
            P(),
            P(("groups", "role", "head"), None),
            P(("groups", "role", "head"), None),
            P(None, ("role", "head")),
            P(None, ("role", "head")),
            P(("role", "head"), None),
        ),
        out_specs=P(("groups", "role", "head"), None),
        check_vma=False,
    )
```

```python
import functools

import jax
import jax.numpy as jnp
from jax import lax
from jax.experimental import pallas as pl
from jax.experimental.pallas import tpu as pltpu
from jax.sharding import PartitionSpec as P

LATENT = 512
ROPE = 64
VDIM = 128
EXPERTS = 8
CAP = 2
F32 = jnp.float32
BF16 = jnp.bfloat16
VMEM = pltpu.VMEM


def slot_of(ids_ref, token, choice):
    mine = ids_ref[choice, token]
    rank = jnp.int32(0)
    choices = ids_ref.shape[0]
    for earlier in range(token * choices + choice):
        rank += (ids_ref[earlier % choices, earlier // choices] == mine).astype(jnp.int32)
    return mine * CAP + rank


def attend_kernel(
    resid_ref, length_hbm, ids_hbm, query_hbm, cache_hbm, value_hbm, weight_hbm, weight_ref, *refs
):
    outs, refs = refs[:-11], refs[-11:]
    query_ref, cache_ref, value_ref, latent_ref, head_ref, side_ref, length_ref, ids_ref = refs[:8]
    cache_sems, value_sems, other_sems = refs[8:]
    requests, heads, _ = query_ref.shape
    groups = value_ref.shape[0]
    per = value_ref.shape[1]
    share, width = resid_ref.shape
    cols = width // len(outs)
    wide = heads * VDIM
    left = outs[0].shape[1] - wide
    role = lax.axis_index("role")
    scalars = [
        pltpu.make_async_copy(ids_hbm, ids_ref, other_sems.at[0]),
        pltpu.make_async_copy(length_hbm, length_ref, other_sems.at[1]),
    ]
    last = pltpu.make_async_copy(weight_hbm, weight_ref, other_sems.at[2])
    copies = [pltpu.make_async_copy(query_hbm, query_ref, other_sems.at[3])]
    for t in range(requests):
        copies.append(pltpu.make_async_copy(cache_hbm.at[t], cache_ref.at[t], cache_sems.at[t]))
    for g in range(groups):
        copies.append(
            pltpu.make_async_copy(
                value_hbm.at[pl.ds(g * per, per)], value_ref.at[g], value_sems.at[g]
            )
        )
    for copy in (*scalars, *copies, last):
        copy.start()
    for copy in scalars:
        copy.wait()

    side_ref[0:share, :width] = resid_ref[...].astype(F32)
    side_ref[share:, :width] = resid_ref[...].astype(F32)
    side_ref[:, width:] = jnp.zeros((2 * share, 128), F32)
    row = lax.broadcasted_iota(jnp.int32, (2 * share, 128), 0)
    lane = lax.broadcasted_iota(jnp.int32, (2 * share, 128), 1)
    notes = jnp.zeros((2 * share, 128), F32)
    for t in range(share):
        for k in range(2):
            slot = slot_of(ids_ref, t, k).astype(F32)
            notes = jnp.where((row == share + t) & (lane == k), slot, notes)
    upper = lax.broadcasted_iota(jnp.int32, (2 * share, left), 0) < share
    for step, out in enumerate(outs):
        start = pl.multiple_of((role ^ step) * cols, 128)
        first = side_ref[:, pl.ds(start, left)]
        second = side_ref[:, pl.ds(start + left, cols - left)]
        second = jnp.concatenate([second, notes], axis=1)
        out[:, wide:] = jnp.where(upper, first, second).astype(BF16)

    scale = (VDIM + ROPE) ** (-0.5)
    for copy in copies[: 1 + requests]:
        copy.wait()
    scores = [
        jnp.dot(query_ref[t], cache_ref[t], preferred_element_type=F32) for t in range(requests)
    ]
    position = lax.broadcasted_iota(jnp.int32, scores[0].shape, 1)
    scores = [
        jnp.where(position < length_ref[t], scores[t] * scale, -jnp.inf) for t in range(requests)
    ]
    tops = [jnp.max(v, axis=1, keepdims=True) for v in scores]
    weights = [jnp.exp(v - top) for v, top in zip(scores, tops)]
    sums = [jnp.sum(v, axis=1, keepdims=True) for v in weights]
    probs = [(v / total).astype(BF16) for v, total in zip(weights, sums)]
    for t in range(requests):
        latent = lax.dot_general(
            probs[t], cache_ref[t, :LATENT], (((1,), (1,)), ((), ())), preferred_element_type=F32
        )
        latent = latent.astype(BF16).astype(F32)
        for c in range(LATENT // 128):
            latent_ref[c, t * heads : (t + 1) * heads, :] = latent[:, c * 128 : (c + 1) * 128]
    for copy in copies[1 + requests :]:
        copy.wait()
    for g in range(groups):
        for i in range(per):
            h = g * per + i
            latent = jnp.concatenate(
                [
                    latent_ref[c, pl.ds(h, requests, stride=heads), :]
                    for c in range(LATENT // 128)
                ],
                axis=1,
            ).astype(BF16)
            head = jnp.dot(latent, value_ref[g, i], preferred_element_type=F32)
            head_ref[:, h * VDIM : (h + 1) * VDIM] = head.astype(BF16)
    for out in outs:
        out[:, :wide] = head_ref[...]
    last.wait()


def attend(lengths, ids, residual, queries, cache, values, weight, roles):
    requests, heads, width = queries.shape
    groups = 4
    hbm = [
        pltpu.with_memory_space_constraint(w, pltpu.HBM)
        for w in (lengths, ids, queries, cache, values, weight)
    ]
    whole = pl.BlockSpec(memory_space=VMEM)
    return pl.pallas_call(
        attend_kernel,
        out_shape=(VMEM(weight.shape, weight.dtype),)
        + (jax.ShapeDtypeStruct((requests, heads * VDIM + 512), BF16),) * roles,
        in_specs=[whole] + [pl.BlockSpec(memory_space=pltpu.HBM)] * 6,
        out_specs=(whole,) * (1 + roles),
        scratch_shapes=[
            VMEM(queries.shape, BF16),
            VMEM(cache.shape, BF16),
            VMEM((groups, heads // groups) + values.shape[1:], BF16),
            VMEM((LATENT // 128, requests * heads, 128), F32),
            VMEM((requests, heads * VDIM), BF16),
            VMEM((2 * residual.shape[0], residual.shape[1] + 128), F32),
            pltpu.SMEM(lengths.shape, jnp.int32),
            pltpu.SMEM(ids.shape, jnp.int32),
            pltpu.SemaphoreType.DMA((requests,)),
            pltpu.SemaphoreType.DMA((groups,)),
            pltpu.SemaphoreType.DMA((4,)),
        ],
        compiler_params=pltpu.CompilerParams(vmem_limit_bytes=24 << 20),
        name="attend",
    )(residual, *hbm)


def combine_kernel(ids_ref, route_ref, received_ref, returned_ref, out_ref, sum_ref):
    roles, slots, _ = received_ref.shape
    share, width = out_ref.shape
    cols = width // roles
    for r in range(roles):
        kept = received_ref[r, :, cols:].astype(F32)
        for g in range(4):
            reach = min(256, cols - g * 256)
            start = r * cols + g * 256
            sum_ref[:, start : start + reach] = kept[g * share : (g + 1) * share, :reach]
    for t in range(share):
        extra = []
        for k in range(2):
            slot = slot_of(ids_ref, t, k)
            both = returned_ref[ids_ref[k, t]].astype(F32)
            one = jnp.where(slot % CAP == 0, both[0:1], both[1:2])
            extra.append(route_ref[k, t] * one)
        sum_ref[t : t + 1, :] += extra[0] + extra[1]
    out_ref[...] = sum_ref[...].astype(BF16)


def combine(ids, route, received, returned, share):
    width = returned.shape[2]
    whole = pl.BlockSpec(memory_space=VMEM)
    scalars = pl.BlockSpec(memory_space=pltpu.SMEM)
    return pl.pallas_call(
        combine_kernel,
        out_shape=jax.ShapeDtypeStruct((share, width), BF16),
        in_specs=[scalars] * 2 + [whole] * 2,
        out_specs=whole,
        scratch_shapes=[VMEM((share, width), F32)],
        compiler_params=pltpu.CompilerParams(vmem_limit_bytes=6 << 20),
        name="combine",
    )(ids, route, received, returned)


def load_kernel(gate_hbm, up_hbm, after_ref, both_ref, sems):
    half = both_ref.shape[2]
    parts = ((gate_hbm, 0), (gate_hbm, half), (up_hbm, 0))
    copies = [
        pltpu.make_async_copy(src.at[:, pl.ds(start, half)], both_ref.at[i], sems.at[i])
        for i, (src, start) in enumerate(parts)
    ]
    for copy in copies:
        copy.start()
    for copy in copies:
        copy.wait()


def load(gate, up, after):
    gate, up = [pltpu.with_memory_space_constraint(w, pltpu.HBM) for w in (gate, up)]
    return pl.pallas_call(
        load_kernel,
        out_shape=VMEM((3, gate.shape[0], gate.shape[1] // 2), gate.dtype),
        in_specs=[pl.BlockSpec(memory_space=pltpu.HBM)] * 2 + [pl.BlockSpec(memory_space=pl.ANY)],
        out_specs=pl.BlockSpec(memory_space=VMEM),
        scratch_shapes=[pltpu.SemaphoreType.DMA((3,))],
        compiler_params=pltpu.CompilerParams(vmem_limit_bytes=1 << 20),
        cost_estimate=pl.CostEstimate(
            flops=0, bytes_accessed=3 * gate.size, transcendentals=0
        ),
        name="load",
    )(gate, up, after)


def project_kernel(weight_ref, *refs):
    messages, out_ref = refs[:-1], refs[-1]
    depth = weight_ref.shape[0]
    rows = jnp.concatenate([m[:, :depth].astype(F32) for m in messages], axis=0).astype(BF16)
    out_ref[...] = jnp.dot(rows, weight_ref[...], preferred_element_type=F32)


def project(messages, weight):
    cols = weight.shape[1]
    tokens = sum(m.shape[0] for m in messages)
    whole = pl.BlockSpec(memory_space=VMEM)
    return pl.pallas_call(
        project_kernel,
        out_shape=jax.ShapeDtypeStruct((tokens, cols), F32),
        in_specs=[whole] * (1 + len(messages)),
        out_specs=whole,
        compiler_params=pltpu.CompilerParams(vmem_limit_bytes=6 << 20),
        name="project",
    )(pltpu.with_memory_space_constraint(weight, VMEM), *messages)


def dispatch_kernel(mine_ref, other_ref, *refs):
    messages, out_ref = refs[:-1], refs[-1]
    role, core = lax.axis_index("role"), lax.axis_index("head")
    roles = len(messages)
    tokens, cols = mine_ref.shape
    each = tokens // roles
    share = each // 2
    wide = messages[0].shape[1]
    left = 4 * 128
    slots = roles * CAP
    firsts, seconds = [], []
    for m in messages:
        side = m[:, wide - left :].astype(F32)
        turned = pltpu.roll(side, share, 0)
        firsts.append(jnp.where(core == 0, side, turned))
        seconds.append(jnp.where(core == 0, turned, side))
    second = jnp.concatenate(seconds, axis=0)
    resid = jnp.concatenate([jnp.concatenate(firsts, axis=0), second[:, : cols - left]], axis=1)
    notes = second[:, cols - left :].T
    attn_out = (mine_ref[...] + other_ref[...]).astype(BF16)
    hidden = (resid + attn_out.astype(F32)).astype(BF16)
    token = lax.broadcasted_iota(jnp.int32, (1, tokens), 1)
    source = role ^ (token // each)
    member = token % each
    row = lax.broadcasted_iota(jnp.int32, (roles * slots, 1), 0)
    dest, slot = row // slots, row % slots
    want = (dest * CAP + slot % CAP).astype(F32)
    placing = (
        (slot // CAP == source)
        & (member // share == core)
        & ((notes[0:1, :] == want) | (notes[1:2, :] == want))
    )
    keeping = (dest == source) & (member == core * share + slot % share)
    placed = jnp.dot(
        jnp.where(placing, 1.0, 0.0).astype(BF16), hidden, preferred_element_type=F32
    ).astype(BF16)
    kept = jnp.dot(jnp.where(keeping, 1.0, 0.0).astype(BF16), hidden, preferred_element_type=F32)
    kept = jnp.concatenate([kept, jnp.zeros((roles * slots, 1024 - cols), F32)], axis=1)
    group = slot // share
    extra = kept[:, :256]
    for g in range(1, 4):
        extra = jnp.where(group == g, kept[:, g * 256 : (g + 1) * 256], extra)
    extra = extra.astype(BF16)
    for d in range(roles):
        out_ref[d, :, :cols] = placed[d * slots : (d + 1) * slots]
        out_ref[d, :, cols:] = extra[d * slots : (d + 1) * slots]


def dispatch(mine, other, messages):
    roles = len(messages)
    cols = mine.shape[1]
    whole = pl.BlockSpec(memory_space=VMEM)
    return pl.pallas_call(
        dispatch_kernel,
        out_shape=jax.ShapeDtypeStruct((roles, roles * CAP, cols + 256), BF16),
        in_specs=[whole] * (2 + roles),
        out_specs=whole,
        compiler_params=pltpu.CompilerParams(vmem_limit_bytes=6 << 20),
        name="dispatch",
    )(mine, other, *messages)


def expert_kernel(
    mine_ref, other_ref, both_ref, up_hbm, down_hbm, keep_ref, send_ref,
    x_ref, act_ref, up_ref, down_ref, sems
):
    rows = mine_ref.shape[0]
    outs, _, broad = down_ref.shape
    half = both_ref.shape[2]

    def fetch(i):
        cols = pl.ds(i * broad, broad)
        return pltpu.make_async_copy(down_hbm.at[:, cols], down_ref.at[i], sems.at[i])

    rest = pltpu.make_async_copy(up_hbm.at[:, pl.ds(half, half)], up_ref, sems.at[outs])
    rest.start()
    fetch(0).start()
    x_ref[:rows, :] = mine_ref[...]
    x_ref[rows:, :] = other_ref[...]
    for i in range(2):
        gate = jnp.dot(x_ref[...], both_ref[i], preferred_element_type=F32)
        if i:
            for j in range(4, outs):
                fetch(j).start()
            up = jnp.dot(x_ref[...], up_ref[...], preferred_element_type=F32)
        else:
            up = jnp.dot(x_ref[...], both_ref[2], preferred_element_type=F32)
            rest.wait()
            for j in range(1, 4):
                fetch(j).start()
        act = (gate / (1.0 + jnp.exp(-gate)) * up).astype(BF16)
        act_ref[:, i * half : (i + 1) * half] = act
    for i in range(outs):
        fetch(i).wait()
        part = jnp.dot(act_ref[...], down_ref[i], preferred_element_type=F32)
        keep_ref[:, i * broad : (i + 1) * broad] = part[:rows]
        send_ref[:, i * broad : (i + 1) * broad] = part[rows:].astype(send_ref.dtype)


def run_experts(mine, other, both, up, down):
    rows, width = mine.shape
    units = up.shape[1]
    outs = 7
    both = pltpu.with_memory_space_constraint(both, VMEM)
    up, down = [pltpu.with_memory_space_constraint(w, pltpu.HBM) for w in (up, down)]
    whole = pl.BlockSpec(memory_space=VMEM)
    return pl.pallas_call(
        expert_kernel,
        out_shape=(
            jax.ShapeDtypeStruct((rows, width), F32),
            jax.ShapeDtypeStruct((rows, width), F32),
        ),
        in_specs=[whole] * 3 + [pl.BlockSpec(memory_space=pltpu.HBM)] * 2,
        out_specs=(whole, whole),
        scratch_shapes=[
            VMEM((2 * rows, width), BF16),
            VMEM((2 * rows, units), BF16),
            VMEM((width, units // 2), BF16),
            VMEM((outs, units, width // outs), BF16),
            pltpu.SemaphoreType.DMA((outs + 1,)),
        ],
        compiler_params=pltpu.CompilerParams(vmem_limit_bytes=26 << 20),
        cost_estimate=pl.CostEstimate(
            flops=12 * rows * width * units, bytes_accessed=3 * width * units, transcendentals=0
        ),
        name="experts",
    )(mine, other, both, up, down)


def norm_kernel(received_ref, gain_ref, out_ref):
    roles = received_ref.shape[0]
    width = out_ref.shape[1]
    cols = width // roles
    total = jnp.float32(0.0)
    for r in range(roles):
        x = received_ref[r, :, :cols].astype(F32)
        total += jnp.sum(x * x, axis=1, keepdims=True)
    inverse = lax.rsqrt(total / width + 1e-06)
    for r in range(roles):
        x = received_ref[r, :, :cols].astype(F32)
        here = slice(r * cols, (r + 1) * cols)
        out_ref[:, here] = (x * inverse * gain_ref[:, here]).astype(BF16)


def normalise(received, gain):
    whole = pl.BlockSpec(memory_space=VMEM)
    return pl.pallas_call(
        norm_kernel,
        out_shape=jax.ShapeDtypeStruct((received.shape[1], gain.shape[1]), BF16),
        in_specs=[whole] * 2,
        out_specs=whole,
        compiler_params=pltpu.CompilerParams(vmem_limit_bytes=4 << 20),
        name="normalise",
    )(received, gain)


def fast(
    queries,
    kv_cache,
    cache_lengths,
    uv_weight,
    out_weight,
    residual,
    norm_gain,
    expert_ids,
    route_weights,
    gate_weight,
    up_weight,
    down_weight,
):
    roles = lax.axis_size("role")
    share = residual.shape[0]
    width = residual.shape[1]
    cols = width // roles
    ids = expert_ids.T
    cache = kv_cache.transpose(0, 2, 1)
    out_weight, *messages = attend(
        cache_lengths, ids, residual, queries, cache, uv_weight, out_weight, roles
    )
    both_weights = load(gate_weight, up_weight, messages[0])
    messages = [messages[0]] + [
        lax.ppermute(messages[step], "role", [(i, i ^ step) for i in range(roles)])
        for step in range(1, roles)
    ]
    messages, both_weights = lax.optimization_barrier((messages, both_weights))
    partial_value = project(messages, out_weight)
    other_value = lax.ppermute(partial_value, "head", [(0, 1), (1, 0)])
    outgoing = dispatch(partial_value, other_value, messages)
    received = lax.all_to_all(outgoing, "role", split_axis=0, concat_axis=0, tiled=True)
    normed = normalise(received, norm_gain.reshape(1, -1))
    other = lax.ppermute(normed, "head", [(0, 1), (1, 0)])
    keep, send = run_experts(normed, other, both_weights, up_weight, down_weight)
    summed = (keep + lax.ppermute(send, "head", [(0, 1), (1, 0)])).astype(BF16)
    returned = lax.all_to_all(
        summed.reshape(roles, CAP, width), "role", split_axis=0, concat_axis=0, tiled=True
    )
    return combine(ids, route_weights.T, received, returned, share)


def attend_general(queries, kv_cache, cache_lengths, uv_weight):
    scale_factor = (VDIM + ROPE) ** (-0.5)
    scores = (
        jnp.einsum("thc,tsc->ths", queries, kv_cache, preferred_element_type=jnp.float32)
        * scale_factor
    )
    position = lax.broadcasted_iota(jnp.int32, scores.shape, 2)
    scores = jnp.where(position < cache_lengths[:, None, None], scores, -jnp.inf)
    top_score = jnp.max(scores, axis=2, keepdims=True)
    weights = jnp.exp(scores - top_score)
    attn_probs = (weights / jnp.sum(weights, axis=2, keepdims=True)).astype(jnp.bfloat16)
    latent_out = jnp.einsum(
        "ths,tsc->thc", attn_probs, kv_cache[:, :, :LATENT], preferred_element_type=jnp.float32
    ).astype(jnp.bfloat16)
    head_out = jnp.einsum(
        "thc,hcv->thv", latent_out, uv_weight, preferred_element_type=jnp.float32
    ).astype(jnp.bfloat16)
    return head_out.reshape(head_out.shape[0], -1)


def general(
    queries,
    kv_cache,
    cache_lengths,
    uv_weight,
    out_weight,
    residual,
    norm_gain,
    expert_ids,
    route_weights,
    gate_weight,
    up_weight,
    down_weight,
):
    role_n = lax.axis_size("role")
    head_n = lax.axis_size("head")
    share_rows = residual.shape[0]
    model_width = residual.shape[1]
    head_out = attend_general(queries, kv_cache, cache_lengths, uv_weight)
    partial_value = jnp.dot(
        lax.all_gather(head_out, "role", axis=0, tiled=True),
        out_weight,
        preferred_element_type=jnp.float32,
    )
    summed_cols = lax.psum(partial_value, "head").astype(jnp.bfloat16)
    own_rows = lax.all_to_all(summed_cols, "role", split_axis=0, concat_axis=1, tiled=True)
    attn_out = lax.dynamic_slice_in_dim(
        own_rows, lax.axis_index("head") * share_rows, share_rows, 0
    )
    hidden = (residual.astype(jnp.float32) + attn_out.astype(jnp.float32)).astype(jnp.bfloat16)
    hidden_f = hidden.astype(jnp.float32)
    inverse = lax.rsqrt(jnp.mean(hidden_f * hidden_f, axis=1, keepdims=True) + 1e-06)
    normed = (hidden_f * inverse * norm_gain[None, :]).astype(jnp.bfloat16)
    flat_ids = expert_ids.reshape(-1)
    onehot = (
        flat_ids[:, None] == lax.broadcasted_iota(jnp.int32, (flat_ids.shape[0], EXPERTS), 1)
    ).astype(jnp.int32)
    slot_rank = jnp.sum(onehot * (jnp.cumsum(onehot, axis=0) - onehot), axis=1).reshape(
        expert_ids.shape
    )
    position = expert_ids * CAP + slot_rank
    slot_grid = lax.broadcasted_iota(jnp.int32, (EXPERTS * CAP,) + expert_ids.shape, 0)
    matches = slot_grid == position[None, :, :]
    placing = jnp.any(matches, axis=2).astype(jnp.bfloat16)
    mixing = jnp.sum(jnp.where(matches, route_weights[None, :, :], 0.0), axis=2).T
    buffer = (
        jnp.dot(placing, normed, preferred_element_type=jnp.float32)
        .astype(jnp.bfloat16)
        .reshape(EXPERTS, CAP, model_width)
    )
    devices = role_n * head_n
    group_size = devices // EXPERTS
    outgoing = jnp.repeat(buffer, group_size, axis=0)
    received = lax.all_to_all(outgoing, ("role", "head"), split_axis=0, concat_axis=0, tiled=True)
    item_count = received.shape[1]
    token_rows = received.reshape(-1, model_width)
    gate_val = jnp.dot(token_rows, gate_weight, preferred_element_type=jnp.float32)
    up_val = jnp.dot(token_rows, up_weight, preferred_element_type=jnp.float32)
    act_val = (jax.nn.silu(gate_val) * up_val).astype(jnp.bfloat16)
    expert_part = jnp.dot(act_val, down_weight, preferred_element_type=jnp.float32).reshape(
        devices, item_count, model_width
    )
    returned = lax.all_to_all(
        expert_part, ("role", "head"), split_axis=0, concat_axis=0, tiled=True
    )
    expert_out = jnp.sum(returned.reshape(EXPERTS, group_size, CAP, model_width), axis=1)
    combined = jnp.dot(
        mixing,
        expert_out.reshape(EXPERTS * CAP, model_width),
        precision=lax.Precision.HIGHEST,
        preferred_element_type=jnp.float32,
    )
    return (hidden_f + combined).astype(jnp.bfloat16)


def on_device(*arrays):
    residual = arrays[5]
    roles = lax.axis_size("role")
    fits = roles == EXPERTS and lax.axis_size("head") == 2 and residual.shape[0] == 4
    return (fast if fits and residual.shape[1] == roles * 896 else general)(*arrays)


def solution(mesh):
    return jax.shard_map(
        on_device,
        mesh=mesh,
        in_specs=(
            P(("groups", "role"), "head", None),
            P(("groups", "role"), None, None),
            P(("groups", "role")),
            P("head", None, None),
            P("head", "role"),
            P(("groups", "role", "head"), None),
            P(),
            P(("groups", "role", "head"), None),
            P(("groups", "role", "head"), None),
            P(None, ("role", "head")),
            P(None, ("role", "head")),
            P(("role", "head"), None),
        ),
        out_specs=P(("groups", "role", "head"), None),
        check_vma=False,
    )
```

```python
import functools

import jax
import jax.numpy as jnp
from jax import lax
from jax.experimental import pallas as pl
from jax.experimental.pallas import tpu as pltpu
from jax.sharding import PartitionSpec as P

LATENT = 512
ROPE = 64
VDIM = 128
EXPERTS = 8
CAP = 2
F32 = jnp.float32
BF16 = jnp.bfloat16
VMEM = pltpu.VMEM


def slot_of(ids_ref, token, choice):
    mine = ids_ref[choice, token]
    rank = jnp.int32(0)
    choices = ids_ref.shape[0]
    for earlier in range(token * choices + choice):
        rank += (ids_ref[earlier % choices, earlier // choices] == mine).astype(jnp.int32)
    return mine * CAP + rank


def attend_kernel(
    resid_ref, length_hbm, ids_hbm, query_hbm, cache_hbm, value_hbm, weight_hbm, weight_ref, *refs
):
    outs, refs = refs[:-11], refs[-11:]
    query_ref, cache_ref, value_ref, latent_ref, head_ref, side_ref, length_ref, ids_ref = refs[:8]
    cache_sems, value_sems, other_sems = refs[8:]
    requests, heads, _ = query_ref.shape
    groups = value_ref.shape[0]
    per = value_ref.shape[1]
    share, width = resid_ref.shape
    cols = width // len(outs)
    wide = heads * VDIM
    left = outs[0].shape[1] - wide
    role = lax.axis_index("role")
    scalars = [
        pltpu.make_async_copy(ids_hbm, ids_ref, other_sems.at[0]),
        pltpu.make_async_copy(length_hbm, length_ref, other_sems.at[1]),
    ]
    last = pltpu.make_async_copy(weight_hbm, weight_ref, other_sems.at[2])
    copies = [pltpu.make_async_copy(query_hbm, query_ref, other_sems.at[3])]
    for t in range(requests):
        copies.append(pltpu.make_async_copy(cache_hbm.at[t], cache_ref.at[t], cache_sems.at[t]))
    for g in range(groups):
        copies.append(
            pltpu.make_async_copy(
                value_hbm.at[pl.ds(g * per, per)], value_ref.at[g], value_sems.at[g]
            )
        )
    for copy in (*scalars, *copies, last):
        copy.start()
    for copy in scalars:
        copy.wait()

    side_ref[0:share, :width] = resid_ref[...].astype(F32)
    side_ref[share:, :width] = resid_ref[...].astype(F32)
    side_ref[:, width:] = jnp.zeros((2 * share, 128), F32)
    row = lax.broadcasted_iota(jnp.int32, (2 * share, 128), 0)
    lane = lax.broadcasted_iota(jnp.int32, (2 * share, 128), 1)
    notes = jnp.zeros((2 * share, 128), F32)
    for t in range(share):
        for k in range(2):
            slot = slot_of(ids_ref, t, k).astype(F32)
            notes = jnp.where((row == share + t) & (lane == k), slot, notes)
    upper = lax.broadcasted_iota(jnp.int32, (2 * share, left), 0) < share
    for step, out in enumerate(outs):
        start = pl.multiple_of((role ^ step) * cols, 128)
        first = side_ref[:, pl.ds(start, left)]
        second = side_ref[:, pl.ds(start + left, cols - left)]
        second = jnp.concatenate([second, notes], axis=1)
        out[:, wide:] = jnp.where(upper, first, second).astype(BF16)

    scale = (VDIM + ROPE) ** (-0.5)
    for copy in copies[: 1 + requests]:
        copy.wait()
    scores = [
        jnp.dot(query_ref[t], cache_ref[t], preferred_element_type=F32) for t in range(requests)
    ]
    position = lax.broadcasted_iota(jnp.int32, scores[0].shape, 1)
    scores = [
        jnp.where(position < length_ref[t], scores[t] * scale, -jnp.inf) for t in range(requests)
    ]
    tops = [jnp.max(v, axis=1, keepdims=True) for v in scores]
    weights = [jnp.exp(v - top) for v, top in zip(scores, tops)]
    sums = [jnp.sum(v, axis=1, keepdims=True) for v in weights]
    probs = [(v / total).astype(BF16) for v, total in zip(weights, sums)]
    for t in range(requests):
        latent = lax.dot_general(
            probs[t], cache_ref[t, :LATENT], (((1,), (1,)), ((), ())), preferred_element_type=F32
        )
        latent = latent.astype(BF16).astype(F32)
        for c in range(LATENT // 128):
            latent_ref[c, t * heads : (t + 1) * heads, :] = latent[:, c * 128 : (c + 1) * 128]
    for copy in copies[1 + requests :]:
        copy.wait()
    for g in range(groups):
        for i in range(per):
            h = g * per + i
            latent = jnp.concatenate(
                [
                    latent_ref[c, pl.ds(h, requests, stride=heads), :]
                    for c in range(LATENT // 128)
                ],
                axis=1,
            ).astype(BF16)
            head = jnp.dot(latent, value_ref[g, i], preferred_element_type=F32)
            head_ref[:, h * VDIM : (h + 1) * VDIM] = head.astype(BF16)
    for out in outs:
        out[:, :wide] = head_ref[...]
    last.wait()


def attend(lengths, ids, residual, queries, cache, values, weight, roles):
    requests, heads, width = queries.shape
    groups = 4
    hbm = [
        pltpu.with_memory_space_constraint(w, pltpu.HBM)
        for w in (lengths, ids, queries, cache, values, weight)
    ]
    whole = pl.BlockSpec(memory_space=VMEM)
    return pl.pallas_call(
        attend_kernel,
        out_shape=(VMEM(weight.shape, weight.dtype),)
        + (jax.ShapeDtypeStruct((requests, heads * VDIM + 512), BF16),) * roles,
        in_specs=[whole] + [pl.BlockSpec(memory_space=pltpu.HBM)] * 6,
        out_specs=(whole,) * (1 + roles),
        scratch_shapes=[
            VMEM(queries.shape, BF16),
            VMEM(cache.shape, BF16),
            VMEM((groups, heads // groups) + values.shape[1:], BF16),
            VMEM((LATENT // 128, requests * heads, 128), F32),
            VMEM((requests, heads * VDIM), BF16),
            VMEM((2 * residual.shape[0], residual.shape[1] + 128), F32),
            pltpu.SMEM(lengths.shape, jnp.int32),
            pltpu.SMEM(ids.shape, jnp.int32),
            pltpu.SemaphoreType.DMA((requests,)),
            pltpu.SemaphoreType.DMA((groups,)),
            pltpu.SemaphoreType.DMA((4,)),
        ],
        compiler_params=pltpu.CompilerParams(vmem_limit_bytes=24 << 20),
        name="attend",
    )(residual, *hbm)


def combine_kernel(ids_ref, route_ref, received_ref, returned_ref, out_ref, sum_ref):
    roles, slots, _ = received_ref.shape
    share, width = out_ref.shape
    cols = width // roles
    for r in range(roles):
        kept = received_ref[r, :, cols:].astype(F32)
        for g in range(4):
            reach = min(256, cols - g * 256)
            start = r * cols + g * 256
            sum_ref[:, start : start + reach] = kept[g * share : (g + 1) * share, :reach]
    for t in range(share):
        extra = []
        for k in range(2):
            slot = slot_of(ids_ref, t, k)
            both = returned_ref[ids_ref[k, t]].astype(F32)
            one = jnp.where(slot % CAP == 0, both[0:1], both[1:2])
            extra.append(route_ref[k, t] * one)
        sum_ref[t : t + 1, :] += extra[0] + extra[1]
    out_ref[...] = sum_ref[...].astype(BF16)


def combine(ids, route, received, returned, share):
    width = returned.shape[2]
    whole = pl.BlockSpec(memory_space=VMEM)
    scalars = pl.BlockSpec(memory_space=pltpu.SMEM)
    return pl.pallas_call(
        combine_kernel,
        out_shape=jax.ShapeDtypeStruct((share, width), BF16),
        in_specs=[scalars] * 2 + [whole] * 2,
        out_specs=whole,
        scratch_shapes=[VMEM((share, width), F32)],
        compiler_params=pltpu.CompilerParams(vmem_limit_bytes=6 << 20),
        name="combine",
    )(ids, route, received, returned)


def load_kernel(gate_hbm, up_hbm, after_ref, both_ref, sems):
    half = both_ref.shape[2]
    parts = ((gate_hbm, 0), (gate_hbm, half), (up_hbm, 0))
    copies = [
        pltpu.make_async_copy(src.at[:, pl.ds(start, half)], both_ref.at[i], sems.at[i])
        for i, (src, start) in enumerate(parts)
    ]
    for copy in copies:
        copy.start()
    for copy in copies:
        copy.wait()


def load(gate, up, after):
    gate, up = [pltpu.with_memory_space_constraint(w, pltpu.HBM) for w in (gate, up)]
    return pl.pallas_call(
        load_kernel,
        out_shape=VMEM((3, gate.shape[0], gate.shape[1] // 2), gate.dtype),
        in_specs=[pl.BlockSpec(memory_space=pltpu.HBM)] * 2 + [pl.BlockSpec(memory_space=pl.ANY)],
        out_specs=pl.BlockSpec(memory_space=VMEM),
        scratch_shapes=[pltpu.SemaphoreType.DMA((3,))],
        compiler_params=pltpu.CompilerParams(vmem_limit_bytes=1 << 20),
        cost_estimate=pl.CostEstimate(
            flops=0, bytes_accessed=3 * gate.size, transcendentals=0
        ),
        name="load",
    )(gate, up, after)


def project_kernel(weight_ref, *refs):
    messages, out_ref = refs[:-1], refs[-1]
    depth = weight_ref.shape[0]
    rows = jnp.concatenate([m[:, :depth].astype(F32) for m in messages], axis=0).astype(BF16)
    out_ref[...] = jnp.dot(rows, weight_ref[...], preferred_element_type=F32)


def project(messages, weight):
    cols = weight.shape[1]
    tokens = sum(m.shape[0] for m in messages)
    whole = pl.BlockSpec(memory_space=VMEM)
    return pl.pallas_call(
        project_kernel,
        out_shape=jax.ShapeDtypeStruct((tokens, cols), F32),
        in_specs=[whole] * (1 + len(messages)),
        out_specs=whole,
        compiler_params=pltpu.CompilerParams(vmem_limit_bytes=6 << 20),
        name="project",
    )(pltpu.with_memory_space_constraint(weight, VMEM), *messages)


def dispatch_kernel(mine_ref, other_ref, *refs):
    messages, out_ref = refs[:-1], refs[-1]
    role, core = lax.axis_index("role"), lax.axis_index("head")
    roles = len(messages)
    tokens, cols = mine_ref.shape
    each = tokens // roles
    share = each // 2
    wide = messages[0].shape[1]
    left = 4 * 128
    slots = roles * CAP
    firsts, seconds = [], []
    for m in messages:
        side = m[:, wide - left :].astype(F32)
        turned = pltpu.roll(side, share, 0)
        firsts.append(jnp.where(core == 0, side, turned))
        seconds.append(jnp.where(core == 0, turned, side))
    second = jnp.concatenate(seconds, axis=0)
    resid = jnp.concatenate([jnp.concatenate(firsts, axis=0), second[:, : cols - left]], axis=1)
    notes = second[:, cols - left :].T
    attn_out = (mine_ref[...] + other_ref[...]).astype(BF16)
    hidden = (resid + attn_out.astype(F32)).astype(BF16)
    token = lax.broadcasted_iota(jnp.int32, (1, tokens), 1)
    source = role ^ (token // each)
    member = token % each
    row = lax.broadcasted_iota(jnp.int32, (roles * slots, 1), 0)
    dest, slot = row // slots, row % slots
    want = (dest * CAP + slot % CAP).astype(F32)
    placing = (
        (slot // CAP == source)
        & (member // share == core)
        & ((notes[0:1, :] == want) | (notes[1:2, :] == want))
    )
    keeping = (dest == source) & (member == core * share + slot % share)
    placed = jnp.dot(
        jnp.where(placing, 1.0, 0.0).astype(BF16), hidden, preferred_element_type=F32
    ).astype(BF16)
    kept = jnp.dot(jnp.where(keeping, 1.0, 0.0).astype(BF16), hidden, preferred_element_type=F32)
    kept = jnp.concatenate([kept, jnp.zeros((roles * slots, 1024 - cols), F32)], axis=1)
    group = slot // share
    extra = kept[:, :256]
    for g in range(1, 4):
        extra = jnp.where(group == g, kept[:, g * 256 : (g + 1) * 256], extra)
    extra = extra.astype(BF16)
    for d in range(roles):
        out_ref[d, :, :cols] = placed[d * slots : (d + 1) * slots]
        out_ref[d, :, cols:] = extra[d * slots : (d + 1) * slots]


def dispatch(mine, other, messages):
    roles = len(messages)
    cols = mine.shape[1]
    whole = pl.BlockSpec(memory_space=VMEM)
    return pl.pallas_call(
        dispatch_kernel,
        out_shape=jax.ShapeDtypeStruct((roles, roles * CAP, cols + 256), BF16),
        in_specs=[whole] * (2 + roles),
        out_specs=whole,
        compiler_params=pltpu.CompilerParams(vmem_limit_bytes=6 << 20),
        name="dispatch",
    )(mine, other, *messages)


def expert_kernel(
    mine_ref, other_ref, both_ref, up_hbm, down_hbm, keep_ref, send_ref,
    x_ref, act_ref, up_ref, down_ref, sems
):
    rows = mine_ref.shape[0]
    outs, _, broad = down_ref.shape
    half = both_ref.shape[2]

    def fetch(i):
        cols = pl.ds(i * broad, broad)
        return pltpu.make_async_copy(down_hbm.at[:, cols], down_ref.at[i], sems.at[i])

    rest = pltpu.make_async_copy(up_hbm.at[:, pl.ds(half, half)], up_ref, sems.at[outs])
    rest.start()
    fetch(0).start()
    x_ref[:rows, :] = mine_ref[...]
    x_ref[rows:, :] = other_ref[...]
    for i in range(2):
        gate = jnp.dot(x_ref[...], both_ref[i], preferred_element_type=F32)
        if i:
            for j in range(4, outs):
                fetch(j).start()
            up = jnp.dot(x_ref[...], up_ref[...], preferred_element_type=F32)
        else:
            up = jnp.dot(x_ref[...], both_ref[2], preferred_element_type=F32)
            rest.wait()
            for j in range(1, 4):
                fetch(j).start()
        act = (gate / (1.0 + jnp.exp(-gate)) * up).astype(BF16)
        act_ref[:, i * half : (i + 1) * half] = act
    for i in range(outs):
        fetch(i).wait()
        part = jnp.dot(act_ref[...], down_ref[i], preferred_element_type=F32)
        keep_ref[:, i * broad : (i + 1) * broad] = part[:rows]
        send_ref[:, i * broad : (i + 1) * broad] = part[rows:].astype(send_ref.dtype)


def run_experts(mine, other, both, up, down):
    rows, width = mine.shape
    units = up.shape[1]
    outs = 7
    both = pltpu.with_memory_space_constraint(both, VMEM)
    up, down = [pltpu.with_memory_space_constraint(w, pltpu.HBM) for w in (up, down)]
    whole = pl.BlockSpec(memory_space=VMEM)
    return pl.pallas_call(
        expert_kernel,
        out_shape=(
            jax.ShapeDtypeStruct((rows, width), F32),
            jax.ShapeDtypeStruct((rows, width), BF16),
        ),
        in_specs=[whole] * 3 + [pl.BlockSpec(memory_space=pltpu.HBM)] * 2,
        out_specs=(whole, whole),
        scratch_shapes=[
            VMEM((2 * rows, width), BF16),
            VMEM((2 * rows, units), BF16),
            VMEM((width, units // 2), BF16),
            VMEM((outs, units, width // outs), BF16),
            pltpu.SemaphoreType.DMA((outs + 1,)),
        ],
        compiler_params=pltpu.CompilerParams(vmem_limit_bytes=26 << 20),
        cost_estimate=pl.CostEstimate(
            flops=12 * rows * width * units, bytes_accessed=3 * width * units, transcendentals=0
        ),
        name="experts",
    )(mine, other, both, up, down)


def norm_kernel(received_ref, gain_ref, out_ref):
    roles = received_ref.shape[0]
    width = out_ref.shape[1]
    cols = width // roles
    total = jnp.float32(0.0)
    for r in range(roles):
        x = received_ref[r, :, :cols].astype(F32)
        total += jnp.sum(x * x, axis=1, keepdims=True)
    inverse = lax.rsqrt(total / width + 1e-06)
    for r in range(roles):
        x = received_ref[r, :, :cols].astype(F32)
        here = slice(r * cols, (r + 1) * cols)
        out_ref[:, here] = (x * inverse * gain_ref[:, here]).astype(BF16)


def normalise(received, gain):
    whole = pl.BlockSpec(memory_space=VMEM)
    return pl.pallas_call(
        norm_kernel,
        out_shape=jax.ShapeDtypeStruct((received.shape[1], gain.shape[1]), BF16),
        in_specs=[whole] * 2,
        out_specs=whole,
        compiler_params=pltpu.CompilerParams(vmem_limit_bytes=4 << 20),
        name="normalise",
    )(received, gain)


def fast(
    queries,
    kv_cache,
    cache_lengths,
    uv_weight,
    out_weight,
    residual,
    norm_gain,
    expert_ids,
    route_weights,
    gate_weight,
    up_weight,
    down_weight,
):
    roles = lax.axis_size("role")
    share = residual.shape[0]
    width = residual.shape[1]
    cols = width // roles
    ids = expert_ids.T
    cache = kv_cache.transpose(0, 2, 1)
    out_weight, *messages = attend(
        cache_lengths, ids, residual, queries, cache, uv_weight, out_weight, roles
    )
    both_weights = load(gate_weight, up_weight, messages[0])
    for step in sorted(range(1, roles), reverse=True):
        pairs = [(i, i ^ step) for i in range(roles)]
        messages[step] = lax.ppermute(messages[step], "role", pairs)
    messages, both_weights = lax.optimization_barrier((messages, both_weights))
    partial_value = project(messages, out_weight)
    other_value = lax.ppermute(partial_value, "head", [(0, 1), (1, 0)])
    outgoing = dispatch(partial_value, other_value, messages)
    received = lax.all_to_all(outgoing, "role", split_axis=0, concat_axis=0, tiled=True)
    normed = normalise(received, norm_gain.reshape(1, -1))
    other = lax.ppermute(normed, "head", [(0, 1), (1, 0)])
    keep, send = run_experts(normed, other, both_weights, up_weight, down_weight)
    sent = lax.ppermute(send, "head", [(0, 1), (1, 0)])
    summed = (keep + sent.astype(F32)).astype(BF16)
    returned = lax.all_to_all(
        summed.reshape(roles, CAP, width), "role", split_axis=0, concat_axis=0, tiled=True
    )
    return combine(ids, route_weights.T, received, returned, share)


def attend_general(queries, kv_cache, cache_lengths, uv_weight):
    scale_factor = (VDIM + ROPE) ** (-0.5)
    scores = (
        jnp.einsum("thc,tsc->ths", queries, kv_cache, preferred_element_type=jnp.float32)
        * scale_factor
    )
    position = lax.broadcasted_iota(jnp.int32, scores.shape, 2)
    scores = jnp.where(position < cache_lengths[:, None, None], scores, -jnp.inf)
    top_score = jnp.max(scores, axis=2, keepdims=True)
    weights = jnp.exp(scores - top_score)
    attn_probs = (weights / jnp.sum(weights, axis=2, keepdims=True)).astype(jnp.bfloat16)
    latent_out = jnp.einsum(
        "ths,tsc->thc", attn_probs, kv_cache[:, :, :LATENT], preferred_element_type=jnp.float32
    ).astype(jnp.bfloat16)
    head_out = jnp.einsum(
        "thc,hcv->thv", latent_out, uv_weight, preferred_element_type=jnp.float32
    ).astype(jnp.bfloat16)
    return head_out.reshape(head_out.shape[0], -1)


def general(
    queries,
    kv_cache,
    cache_lengths,
    uv_weight,
    out_weight,
    residual,
    norm_gain,
    expert_ids,
    route_weights,
    gate_weight,
    up_weight,
    down_weight,
):
    role_n = lax.axis_size("role")
    head_n = lax.axis_size("head")
    share_rows = residual.shape[0]
    model_width = residual.shape[1]
    head_out = attend_general(queries, kv_cache, cache_lengths, uv_weight)
    partial_value = jnp.dot(
        lax.all_gather(head_out, "role", axis=0, tiled=True),
        out_weight,
        preferred_element_type=jnp.float32,
    )
    summed_cols = lax.psum(partial_value, "head").astype(jnp.bfloat16)
    own_rows = lax.all_to_all(summed_cols, "role", split_axis=0, concat_axis=1, tiled=True)
    attn_out = lax.dynamic_slice_in_dim(
        own_rows, lax.axis_index("head") * share_rows, share_rows, 0
    )
    hidden = (residual.astype(jnp.float32) + attn_out.astype(jnp.float32)).astype(jnp.bfloat16)
    hidden_f = hidden.astype(jnp.float32)
    inverse = lax.rsqrt(jnp.mean(hidden_f * hidden_f, axis=1, keepdims=True) + 1e-06)
    normed = (hidden_f * inverse * norm_gain[None, :]).astype(jnp.bfloat16)
    flat_ids = expert_ids.reshape(-1)
    onehot = (
        flat_ids[:, None] == lax.broadcasted_iota(jnp.int32, (flat_ids.shape[0], EXPERTS), 1)
    ).astype(jnp.int32)
    slot_rank = jnp.sum(onehot * (jnp.cumsum(onehot, axis=0) - onehot), axis=1).reshape(
        expert_ids.shape
    )
    position = expert_ids * CAP + slot_rank
    slot_grid = lax.broadcasted_iota(jnp.int32, (EXPERTS * CAP,) + expert_ids.shape, 0)
    matches = slot_grid == position[None, :, :]
    placing = jnp.any(matches, axis=2).astype(jnp.bfloat16)
    mixing = jnp.sum(jnp.where(matches, route_weights[None, :, :], 0.0), axis=2).T
    buffer = (
        jnp.dot(placing, normed, preferred_element_type=jnp.float32)
        .astype(jnp.bfloat16)
        .reshape(EXPERTS, CAP, model_width)
    )
    devices = role_n * head_n
    group_size = devices // EXPERTS
    outgoing = jnp.repeat(buffer, group_size, axis=0)
    received = lax.all_to_all(outgoing, ("role", "head"), split_axis=0, concat_axis=0, tiled=True)
    item_count = received.shape[1]
    token_rows = received.reshape(-1, model_width)
    gate_val = jnp.dot(token_rows, gate_weight, preferred_element_type=jnp.float32)
    up_val = jnp.dot(token_rows, up_weight, preferred_element_type=jnp.float32)
    act_val = (jax.nn.silu(gate_val) * up_val).astype(jnp.bfloat16)
    expert_part = jnp.dot(act_val, down_weight, preferred_element_type=jnp.float32).reshape(
        devices, item_count, model_width
    )
    returned = lax.all_to_all(
        expert_part, ("role", "head"), split_axis=0, concat_axis=0, tiled=True
    )
    expert_out = jnp.sum(returned.reshape(EXPERTS, group_size, CAP, model_width), axis=1)
    combined = jnp.dot(
        mixing,
        expert_out.reshape(EXPERTS * CAP, model_width),
        precision=lax.Precision.HIGHEST,
        preferred_element_type=jnp.float32,
    )
    return (hidden_f + combined).astype(jnp.bfloat16)


def on_device(*arrays):
    residual = arrays[5]
    roles = lax.axis_size("role")
    fits = roles == EXPERTS and lax.axis_size("head") == 2 and residual.shape[0] == 4
    return (fast if fits and residual.shape[1] == roles * 896 else general)(*arrays)


def solution(mesh):
    return jax.shard_map(
        on_device,
        mesh=mesh,
        in_specs=(
            P(("groups", "role"), "head", None),
            P(("groups", "role"), None, None),
            P(("groups", "role")),
            P("head", None, None),
            P("head", "role"),
            P(("groups", "role", "head"), None),
            P(),
            P(("groups", "role", "head"), None),
            P(("groups", "role", "head"), None),
            P(None, ("role", "head")),
            P(None, ("role", "head")),
            P(("role", "head"), None),
        ),
        out_specs=P(("groups", "role", "head"), None),
        check_vma=False,
    )
```

```python
import functools

import jax
import jax.numpy as jnp
from jax import lax
from jax.experimental import pallas as pl
from jax.experimental.pallas import tpu as pltpu
from jax.sharding import PartitionSpec as P

LATENT = 512
ROPE = 64
VDIM = 128
EXPERTS = 8
CAP = 2
F32 = jnp.float32
BF16 = jnp.bfloat16
VMEM = pltpu.VMEM


def slot_of(ids_ref, token, choice):
    mine = ids_ref[choice, token]
    rank = jnp.int32(0)
    choices = ids_ref.shape[0]
    for earlier in range(token * choices + choice):
        rank += (ids_ref[earlier % choices, earlier // choices] == mine).astype(jnp.int32)
    return mine * CAP + rank


def attend_kernel(
    resid_ref, length_hbm, ids_hbm, query_hbm, cache_hbm, value_hbm, weight_hbm, weight_ref, *refs
):
    outs, refs = refs[:-11], refs[-11:]
    query_ref, cache_ref, value_ref, latent_ref, head_ref, side_ref, length_ref, ids_ref = refs[:8]
    cache_sems, value_sems, other_sems = refs[8:]
    requests, heads, _ = query_ref.shape
    groups = value_ref.shape[0]
    per = value_ref.shape[1]
    share, width = resid_ref.shape
    cols = width // len(outs)
    wide = heads * VDIM
    left = outs[0].shape[1] - wide
    role = lax.axis_index("role")
    scalars = [
        pltpu.make_async_copy(ids_hbm, ids_ref, other_sems.at[0]),
        pltpu.make_async_copy(length_hbm, length_ref, other_sems.at[1]),
    ]
    last = pltpu.make_async_copy(weight_hbm, weight_ref, other_sems.at[2])
    copies = [pltpu.make_async_copy(query_hbm, query_ref, other_sems.at[3])]
    for t in range(requests):
        copies.append(pltpu.make_async_copy(cache_hbm.at[t], cache_ref.at[t], cache_sems.at[t]))
    for g in range(groups):
        copies.append(
            pltpu.make_async_copy(
                value_hbm.at[pl.ds(g * per, per)], value_ref.at[g], value_sems.at[g]
            )
        )
    for copy in (*scalars, *copies, last):
        copy.start()
    for copy in scalars:
        copy.wait()

    side_ref[0:share, :width] = resid_ref[...].astype(F32)
    side_ref[share:, :width] = resid_ref[...].astype(F32)
    side_ref[:, width:] = jnp.zeros((2 * share, 128), F32)
    row = lax.broadcasted_iota(jnp.int32, (2 * share, 128), 0)
    lane = lax.broadcasted_iota(jnp.int32, (2 * share, 128), 1)
    notes = jnp.zeros((2 * share, 128), F32)
    for t in range(share):
        for k in range(2):
            slot = slot_of(ids_ref, t, k).astype(F32)
            notes = jnp.where((row == share + t) & (lane == k), slot, notes)
    upper = lax.broadcasted_iota(jnp.int32, (2 * share, left), 0) < share
    for step, out in enumerate(outs):
        start = pl.multiple_of((role ^ step) * cols, 128)
        first = side_ref[:, pl.ds(start, left)]
        second = side_ref[:, pl.ds(start + left, cols - left)]
        second = jnp.concatenate([second, notes], axis=1)
        out[:, wide:] = jnp.where(upper, first, second).astype(BF16)

    scale = (VDIM + ROPE) ** (-0.5)
    for copy in copies[: 1 + requests]:
        copy.wait()
    scores = [
        jnp.dot(query_ref[t], cache_ref[t], preferred_element_type=F32) for t in range(requests)
    ]
    position = lax.broadcasted_iota(jnp.int32, scores[0].shape, 1)
    scores = [
        jnp.where(position < length_ref[t], scores[t] * scale, -jnp.inf) for t in range(requests)
    ]
    tops = [jnp.max(v, axis=1, keepdims=True) for v in scores]
    weights = [jnp.exp(v - top) for v, top in zip(scores, tops)]
    sums = [jnp.sum(v, axis=1, keepdims=True) for v in weights]
    probs = [(v / total).astype(BF16) for v, total in zip(weights, sums)]
    for t in range(requests):
        latent = lax.dot_general(
            probs[t], cache_ref[t, :LATENT], (((1,), (1,)), ((), ())), preferred_element_type=F32
        )
        latent = latent.astype(BF16).astype(F32)
        for c in range(LATENT // 128):
            latent_ref[c, t * heads : (t + 1) * heads, :] = latent[:, c * 128 : (c + 1) * 128]
    for copy in copies[1 + requests :]:
        copy.wait()
    for g in range(groups):
        for i in range(per):
            h = g * per + i
            latent = jnp.concatenate(
                [
                    latent_ref[c, pl.ds(h, requests, stride=heads), :]
                    for c in range(LATENT // 128)
                ],
                axis=1,
            ).astype(BF16)
            head = jnp.dot(latent, value_ref[g, i], preferred_element_type=F32)
            head_ref[:, h * VDIM : (h + 1) * VDIM] = head.astype(BF16)
    for out in outs:
        out[:, :wide] = head_ref[...]
    last.wait()


def attend(lengths, ids, residual, queries, cache, values, weight, roles):
    requests, heads, width = queries.shape
    groups = 4
    hbm = [
        pltpu.with_memory_space_constraint(w, pltpu.HBM)
        for w in (lengths, ids, queries, cache, values, weight)
    ]
    whole = pl.BlockSpec(memory_space=VMEM)
    return pl.pallas_call(
        attend_kernel,
        out_shape=(VMEM(weight.shape, weight.dtype),)
        + (jax.ShapeDtypeStruct((requests, heads * VDIM + 512), BF16),) * roles,
        in_specs=[whole] + [pl.BlockSpec(memory_space=pltpu.HBM)] * 6,
        out_specs=(whole,) * (1 + roles),
        scratch_shapes=[
            VMEM(queries.shape, BF16),
            VMEM(cache.shape, BF16),
            VMEM((groups, heads // groups) + values.shape[1:], BF16),
            VMEM((LATENT // 128, requests * heads, 128), F32),
            VMEM((requests, heads * VDIM), BF16),
            VMEM((2 * residual.shape[0], residual.shape[1] + 128), F32),
            pltpu.SMEM(lengths.shape, jnp.int32),
            pltpu.SMEM(ids.shape, jnp.int32),
            pltpu.SemaphoreType.DMA((requests,)),
            pltpu.SemaphoreType.DMA((groups,)),
            pltpu.SemaphoreType.DMA((4,)),
        ],
        compiler_params=pltpu.CompilerParams(vmem_limit_bytes=24 << 20),
        name="attend",
    )(residual, *hbm)


def combine_kernel(ids_ref, route_ref, received_ref, returned_ref, out_ref, sum_ref):
    roles, slots, _ = received_ref.shape
    share, width = out_ref.shape
    cols = width // roles
    for r in range(roles):
        kept = received_ref[r, :, cols:].astype(F32)
        for g in range(4):
            reach = min(256, cols - g * 256)
            start = r * cols + g * 256
            sum_ref[:, start : start + reach] = kept[g * share : (g + 1) * share, :reach]
    row = lax.broadcasted_iota(jnp.int32, (CAP, 1), 0)
    for t in range(share):
        pair = None
        for k in range(2):
            slot = slot_of(ids_ref, t, k)
            weight = jnp.where(row == slot % CAP, route_ref[k, t], 0.0)
            term = weight * returned_ref[ids_ref[k, t]].astype(F32)
            pair = term if pair is None else pair + term
        sum_ref[t : t + 1, :] += pair[0:1] + pair[1:2]
    out_ref[...] = sum_ref[...].astype(BF16)


def combine(ids, route, received, returned, share):
    width = returned.shape[2]
    whole = pl.BlockSpec(memory_space=VMEM)
    scalars = pl.BlockSpec(memory_space=pltpu.SMEM)
    return pl.pallas_call(
        combine_kernel,
        out_shape=jax.ShapeDtypeStruct((share, width), BF16),
        in_specs=[scalars] * 2 + [whole] * 2,
        out_specs=whole,
        scratch_shapes=[VMEM((share, width), F32)],
        compiler_params=pltpu.CompilerParams(vmem_limit_bytes=6 << 20),
        name="combine",
    )(ids, route, received, returned)


def load_kernel(gate_hbm, up_hbm, after_ref, both_ref, sems):
    half = both_ref.shape[2]
    parts = ((gate_hbm, 0), (gate_hbm, half), (up_hbm, 0))
    copies = [
        pltpu.make_async_copy(src.at[:, pl.ds(start, half)], both_ref.at[i], sems.at[i])
        for i, (src, start) in enumerate(parts)
    ]
    for copy in copies:
        copy.start()
    for copy in copies:
        copy.wait()


def load(gate, up, after):
    gate, up = [pltpu.with_memory_space_constraint(w, pltpu.HBM) for w in (gate, up)]
    return pl.pallas_call(
        load_kernel,
        out_shape=VMEM((3, gate.shape[0], gate.shape[1] // 2), gate.dtype),
        in_specs=[pl.BlockSpec(memory_space=pltpu.HBM)] * 2 + [pl.BlockSpec(memory_space=pl.ANY)],
        out_specs=pl.BlockSpec(memory_space=VMEM),
        scratch_shapes=[pltpu.SemaphoreType.DMA((3,))],
        compiler_params=pltpu.CompilerParams(vmem_limit_bytes=1 << 20),
        cost_estimate=pl.CostEstimate(
            flops=0, bytes_accessed=3 * gate.size, transcendentals=0
        ),
        name="load",
    )(gate, up, after)


def project_kernel(weight_ref, *refs):
    messages, out_ref = refs[:-1], refs[-1]
    depth = weight_ref.shape[0]
    rows = jnp.concatenate([m[:, :depth].astype(F32) for m in messages], axis=0).astype(BF16)
    out_ref[...] = jnp.dot(rows, weight_ref[...], preferred_element_type=F32)


def project(messages, weight):
    cols = weight.shape[1]
    tokens = sum(m.shape[0] for m in messages)
    whole = pl.BlockSpec(memory_space=VMEM)
    return pl.pallas_call(
        project_kernel,
        out_shape=jax.ShapeDtypeStruct((tokens, cols), F32),
        in_specs=[whole] * (1 + len(messages)),
        out_specs=whole,
        compiler_params=pltpu.CompilerParams(vmem_limit_bytes=6 << 20),
        name="project",
    )(pltpu.with_memory_space_constraint(weight, VMEM), *messages)


def dispatch_kernel(mine_ref, other_ref, *refs):
    messages, out_ref = refs[:-1], refs[-1]
    role, core = lax.axis_index("role"), lax.axis_index("head")
    roles = len(messages)
    tokens, cols = mine_ref.shape
    each = tokens // roles
    share = each // 2
    wide = messages[0].shape[1]
    left = 4 * 128
    slots = roles * CAP
    firsts, seconds = [], []
    for m in messages:
        side = m[:, wide - left :].astype(F32)
        turned = pltpu.roll(side, share, 0)
        firsts.append(jnp.where(core == 0, side, turned))
        seconds.append(jnp.where(core == 0, turned, side))
    second = jnp.concatenate(seconds, axis=0)
    resid = jnp.concatenate([jnp.concatenate(firsts, axis=0), second[:, : cols - left]], axis=1)
    notes = second[:, cols - left :].T
    attn_out = (mine_ref[...] + other_ref[...]).astype(BF16)
    hidden = (resid + attn_out.astype(F32)).astype(BF16)
    token = lax.broadcasted_iota(jnp.int32, (1, tokens), 1)
    source = role ^ (token // each)
    member = token % each
    row = lax.broadcasted_iota(jnp.int32, (roles * slots, 1), 0)
    dest, slot = row // slots, row % slots
    want = (dest * CAP + slot % CAP).astype(F32)
    placing = (
        (slot // CAP == source)
        & (member // share == core)
        & ((notes[0:1, :] == want) | (notes[1:2, :] == want))
    )
    keeping = (dest == source) & (member == core * share + slot % share)
    placed = jnp.dot(
        jnp.where(placing, 1.0, 0.0).astype(BF16), hidden, preferred_element_type=F32
    ).astype(BF16)
    kept = jnp.dot(jnp.where(keeping, 1.0, 0.0).astype(BF16), hidden, preferred_element_type=F32)
    kept = jnp.concatenate([kept, jnp.zeros((roles * slots, 1024 - cols), F32)], axis=1)
    group = slot // share
    extra = kept[:, :256]
    for g in range(1, 4):
        extra = jnp.where(group == g, kept[:, g * 256 : (g + 1) * 256], extra)
    extra = extra.astype(BF16)
    for d in range(roles):
        out_ref[d, :, :cols] = placed[d * slots : (d + 1) * slots]
        out_ref[d, :, cols:] = extra[d * slots : (d + 1) * slots]


def dispatch(mine, other, messages):
    roles = len(messages)
    cols = mine.shape[1]
    whole = pl.BlockSpec(memory_space=VMEM)
    return pl.pallas_call(
        dispatch_kernel,
        out_shape=jax.ShapeDtypeStruct((roles, roles * CAP, cols + 256), BF16),
        in_specs=[whole] * (2 + roles),
        out_specs=whole,
        compiler_params=pltpu.CompilerParams(vmem_limit_bytes=6 << 20),
        name="dispatch",
    )(mine, other, *messages)


def expert_kernel(
    mine_ref, other_ref, both_ref, up_hbm, down_hbm, keep_ref, send_ref,
    x_ref, act_ref, up_ref, down_ref, sems
):
    rows = mine_ref.shape[0]
    outs, _, broad = down_ref.shape
    half = both_ref.shape[2]

    def fetch(i):
        cols = pl.ds(i * broad, broad)
        return pltpu.make_async_copy(down_hbm.at[:, cols], down_ref.at[i], sems.at[i])

    rest = pltpu.make_async_copy(up_hbm.at[:, pl.ds(half, half)], up_ref, sems.at[outs])
    rest.start()
    fetch(0).start()
    x_ref[:rows, :] = mine_ref[...]
    x_ref[rows:, :] = other_ref[...]
    for i in range(2):
        gate = jnp.dot(x_ref[...], both_ref[i], preferred_element_type=F32)
        if i:
            for j in range(4, outs):
                fetch(j).start()
            up = jnp.dot(x_ref[...], up_ref[...], preferred_element_type=F32)
        else:
            up = jnp.dot(x_ref[...], both_ref[2], preferred_element_type=F32)
            rest.wait()
            for j in range(1, 4):
                fetch(j).start()
        act = (gate / (1.0 + jnp.exp(-gate)) * up).astype(BF16)
        act_ref[:, i * half : (i + 1) * half] = act
    for i in range(outs):
        fetch(i).wait()
        part = jnp.dot(act_ref[...], down_ref[i], preferred_element_type=F32)
        keep_ref[:, i * broad : (i + 1) * broad] = part[:rows]
        send_ref[:, i * broad : (i + 1) * broad] = part[rows:].astype(send_ref.dtype)


def run_experts(mine, other, both, up, down):
    rows, width = mine.shape
    units = up.shape[1]
    outs = 7
    both = pltpu.with_memory_space_constraint(both, VMEM)
    up, down = [pltpu.with_memory_space_constraint(w, pltpu.HBM) for w in (up, down)]
    whole = pl.BlockSpec(memory_space=VMEM)
    return pl.pallas_call(
        expert_kernel,
        out_shape=(
            jax.ShapeDtypeStruct((rows, width), F32),
            jax.ShapeDtypeStruct((rows, width), BF16),
        ),
        in_specs=[whole] * 3 + [pl.BlockSpec(memory_space=pltpu.HBM)] * 2,
        out_specs=(whole, whole),
        scratch_shapes=[
            VMEM((2 * rows, width), BF16),
            VMEM((2 * rows, units), BF16),
            VMEM((width, units // 2), BF16),
            VMEM((outs, units, width // outs), BF16),
            pltpu.SemaphoreType.DMA((outs + 1,)),
        ],
        compiler_params=pltpu.CompilerParams(vmem_limit_bytes=26 << 20),
        cost_estimate=pl.CostEstimate(
            flops=12 * rows * width * units, bytes_accessed=3 * width * units, transcendentals=0
        ),
        name="experts",
    )(mine, other, both, up, down)


def norm_kernel(received_ref, gain_ref, out_ref):
    roles = received_ref.shape[0]
    width = out_ref.shape[1]
    cols = width // roles
    total = jnp.float32(0.0)
    for r in range(roles):
        x = received_ref[r, :, :cols].astype(F32)
        total += jnp.sum(x * x, axis=1, keepdims=True)
    inverse = lax.rsqrt(total / width + 1e-06)
    for r in range(roles):
        x = received_ref[r, :, :cols].astype(F32)
        here = slice(r * cols, (r + 1) * cols)
        out_ref[:, here] = (x * inverse * gain_ref[:, here]).astype(BF16)


def normalise(received, gain):
    whole = pl.BlockSpec(memory_space=VMEM)
    return pl.pallas_call(
        norm_kernel,
        out_shape=jax.ShapeDtypeStruct((received.shape[1], gain.shape[1]), BF16),
        in_specs=[whole] * 2,
        out_specs=whole,
        compiler_params=pltpu.CompilerParams(vmem_limit_bytes=4 << 20),
        name="normalise",
    )(received, gain)


def fast(
    queries,
    kv_cache,
    cache_lengths,
    uv_weight,
    out_weight,
    residual,
    norm_gain,
    expert_ids,
    route_weights,
    gate_weight,
    up_weight,
    down_weight,
):
    roles = lax.axis_size("role")
    share = residual.shape[0]
    width = residual.shape[1]
    cols = width // roles
    ids = expert_ids.T
    cache = kv_cache.transpose(0, 2, 1)
    out_weight, *messages = attend(
        cache_lengths, ids, residual, queries, cache, uv_weight, out_weight, roles
    )
    both_weights = load(gate_weight, up_weight, messages[0])
    for step in sorted(range(1, roles), reverse=True):
        pairs = [(i, i ^ step) for i in range(roles)]
        messages[step] = lax.ppermute(messages[step], "role", pairs)
    messages, both_weights = lax.optimization_barrier((messages, both_weights))
    partial_value = project(messages, out_weight)
    other_value = lax.ppermute(partial_value, "head", [(0, 1), (1, 0)])
    outgoing = dispatch(partial_value, other_value, messages)
    received = lax.all_to_all(outgoing, "role", split_axis=0, concat_axis=0, tiled=True)
    normed = normalise(received, norm_gain.reshape(1, -1))
    other = lax.ppermute(normed, "head", [(0, 1), (1, 0)])
    keep, send = run_experts(normed, other, both_weights, up_weight, down_weight)
    sent = lax.ppermute(send, "head", [(0, 1), (1, 0)])
    summed = (keep + sent.astype(F32)).astype(BF16)
    returned = lax.all_to_all(
        summed.reshape(roles, CAP, width), "role", split_axis=0, concat_axis=0, tiled=True
    )
    return combine(ids, route_weights.T, received, returned, share)


def attend_general(queries, kv_cache, cache_lengths, uv_weight):
    scale_factor = (VDIM + ROPE) ** (-0.5)
    scores = (
        jnp.einsum("thc,tsc->ths", queries, kv_cache, preferred_element_type=jnp.float32)
        * scale_factor
    )
    position = lax.broadcasted_iota(jnp.int32, scores.shape, 2)
    scores = jnp.where(position < cache_lengths[:, None, None], scores, -jnp.inf)
    top_score = jnp.max(scores, axis=2, keepdims=True)
    weights = jnp.exp(scores - top_score)
    attn_probs = (weights / jnp.sum(weights, axis=2, keepdims=True)).astype(jnp.bfloat16)
    latent_out = jnp.einsum(
        "ths,tsc->thc", attn_probs, kv_cache[:, :, :LATENT], preferred_element_type=jnp.float32
    ).astype(jnp.bfloat16)
    head_out = jnp.einsum(
        "thc,hcv->thv", latent_out, uv_weight, preferred_element_type=jnp.float32
    ).astype(jnp.bfloat16)
    return head_out.reshape(head_out.shape[0], -1)


def general(
    queries,
    kv_cache,
    cache_lengths,
    uv_weight,
    out_weight,
    residual,
    norm_gain,
    expert_ids,
    route_weights,
    gate_weight,
    up_weight,
    down_weight,
):
    role_n = lax.axis_size("role")
    head_n = lax.axis_size("head")
    share_rows = residual.shape[0]
    model_width = residual.shape[1]
    head_out = attend_general(queries, kv_cache, cache_lengths, uv_weight)
    partial_value = jnp.dot(
        lax.all_gather(head_out, "role", axis=0, tiled=True),
        out_weight,
        preferred_element_type=jnp.float32,
    )
    summed_cols = lax.psum(partial_value, "head").astype(jnp.bfloat16)
    own_rows = lax.all_to_all(summed_cols, "role", split_axis=0, concat_axis=1, tiled=True)
    attn_out = lax.dynamic_slice_in_dim(
        own_rows, lax.axis_index("head") * share_rows, share_rows, 0
    )
    hidden = (residual.astype(jnp.float32) + attn_out.astype(jnp.float32)).astype(jnp.bfloat16)
    hidden_f = hidden.astype(jnp.float32)
    inverse = lax.rsqrt(jnp.mean(hidden_f * hidden_f, axis=1, keepdims=True) + 1e-06)
    normed = (hidden_f * inverse * norm_gain[None, :]).astype(jnp.bfloat16)
    flat_ids = expert_ids.reshape(-1)
    onehot = (
        flat_ids[:, None] == lax.broadcasted_iota(jnp.int32, (flat_ids.shape[0], EXPERTS), 1)
    ).astype(jnp.int32)
    slot_rank = jnp.sum(onehot * (jnp.cumsum(onehot, axis=0) - onehot), axis=1).reshape(
        expert_ids.shape
    )
    position = expert_ids * CAP + slot_rank
    slot_grid = lax.broadcasted_iota(jnp.int32, (EXPERTS * CAP,) + expert_ids.shape, 0)
    matches = slot_grid == position[None, :, :]
    placing = jnp.any(matches, axis=2).astype(jnp.bfloat16)
    mixing = jnp.sum(jnp.where(matches, route_weights[None, :, :], 0.0), axis=2).T
    buffer = (
        jnp.dot(placing, normed, preferred_element_type=jnp.float32)
        .astype(jnp.bfloat16)
        .reshape(EXPERTS, CAP, model_width)
    )
    devices = role_n * head_n
    group_size = devices // EXPERTS
    outgoing = jnp.repeat(buffer, group_size, axis=0)
    received = lax.all_to_all(outgoing, ("role", "head"), split_axis=0, concat_axis=0, tiled=True)
    item_count = received.shape[1]
    token_rows = received.reshape(-1, model_width)
    gate_val = jnp.dot(token_rows, gate_weight, preferred_element_type=jnp.float32)
    up_val = jnp.dot(token_rows, up_weight, preferred_element_type=jnp.float32)
    act_val = (jax.nn.silu(gate_val) * up_val).astype(jnp.bfloat16)
    expert_part = jnp.dot(act_val, down_weight, preferred_element_type=jnp.float32).reshape(
        devices, item_count, model_width
    )
    returned = lax.all_to_all(
        expert_part, ("role", "head"), split_axis=0, concat_axis=0, tiled=True
    )
    expert_out = jnp.sum(returned.reshape(EXPERTS, group_size, CAP, model_width), axis=1)
    combined = jnp.dot(
        mixing,
        expert_out.reshape(EXPERTS * CAP, model_width),
        precision=lax.Precision.HIGHEST,
        preferred_element_type=jnp.float32,
    )
    return (hidden_f + combined).astype(jnp.bfloat16)


def on_device(*arrays):
    residual = arrays[5]
    roles = lax.axis_size("role")
    fits = roles == EXPERTS and lax.axis_size("head") == 2 and residual.shape[0] == 4
    return (fast if fits and residual.shape[1] == roles * 896 else general)(*arrays)


def solution(mesh):
    return jax.shard_map(
        on_device,
        mesh=mesh,
        in_specs=(
            P(("groups", "role"), "head", None),
            P(("groups", "role"), None, None),
            P(("groups", "role")),
            P("head", None, None),
            P("head", "role"),
            P(("groups", "role", "head"), None),
            P(),
            P(("groups", "role", "head"), None),
            P(("groups", "role", "head"), None),
            P(None, ("role", "head")),
            P(None, ("role", "head")),
            P(("role", "head"), None),
        ),
        out_specs=P(("groups", "role", "head"), None),
        check_vma=False,
    )
```

```python
import functools

import jax
import jax.numpy as jnp
from jax import lax
from jax.experimental import pallas as pl
from jax.experimental.pallas import tpu as pltpu
from jax.sharding import PartitionSpec as P

LATENT = 512
ROPE = 64
VDIM = 128
EXPERTS = 8
CAP = 2
F32 = jnp.float32
BF16 = jnp.bfloat16
VMEM = pltpu.VMEM


def slot_of(ids_ref, token, choice):
    mine = ids_ref[choice, token]
    rank = jnp.int32(0)
    choices = ids_ref.shape[0]
    for earlier in range(token * choices + choice):
        rank += (ids_ref[earlier % choices, earlier // choices] == mine).astype(jnp.int32)
    return mine * CAP + rank


def attend_kernel(
    resid_ref, length_hbm, ids_hbm, query_hbm, cache_hbm, value_hbm, weight_hbm, weight_ref, *refs
):
    outs, refs = refs[:-11], refs[-11:]
    query_ref, cache_ref, value_ref, latent_ref, head_ref, side_ref, length_ref, ids_ref = refs[:8]
    cache_sems, value_sems, other_sems = refs[8:]
    requests, heads, _ = query_ref.shape
    groups = value_ref.shape[0]
    per = value_ref.shape[1]
    share, width = resid_ref.shape
    cols = width // len(outs)
    wide = heads * VDIM
    left = outs[0].shape[1] - wide
    role = lax.axis_index("role")
    scalars = [
        pltpu.make_async_copy(ids_hbm, ids_ref, other_sems.at[0]),
        pltpu.make_async_copy(length_hbm, length_ref, other_sems.at[1]),
    ]
    last = pltpu.make_async_copy(weight_hbm, weight_ref, other_sems.at[2])
    copies = [pltpu.make_async_copy(query_hbm, query_ref, other_sems.at[3])]
    for t in range(requests):
        copies.append(pltpu.make_async_copy(cache_hbm.at[t], cache_ref.at[t], cache_sems.at[t]))
    for g in range(groups):
        copies.append(
            pltpu.make_async_copy(
                value_hbm.at[pl.ds(g * per, per)], value_ref.at[g], value_sems.at[g]
            )
        )
    for copy in (*scalars, *copies, last):
        copy.start()
    for copy in scalars:
        copy.wait()

    side_ref[0:share, :width] = resid_ref[...].astype(F32)
    side_ref[share:, :width] = resid_ref[...].astype(F32)
    side_ref[:, width:] = jnp.zeros((2 * share, 128), F32)
    row = lax.broadcasted_iota(jnp.int32, (2 * share, 128), 0)
    lane = lax.broadcasted_iota(jnp.int32, (2 * share, 128), 1)
    notes = jnp.zeros((2 * share, 128), F32)
    for t in range(share):
        for k in range(2):
            slot = slot_of(ids_ref, t, k).astype(F32)
            notes = jnp.where((row == share + t) & (lane == k), slot, notes)
    upper = lax.broadcasted_iota(jnp.int32, (2 * share, left), 0) < share
    for step, out in enumerate(outs):
        start = pl.multiple_of((role ^ step) * cols, 128)
        first = side_ref[:, pl.ds(start, left)]
        second = side_ref[:, pl.ds(start + left, cols - left)]
        second = jnp.concatenate([second, notes], axis=1)
        out[:, wide:] = jnp.where(upper, first, second).astype(BF16)

    scale = (VDIM + ROPE) ** (-0.5)
    for copy in copies[: 1 + requests]:
        copy.wait()
    scores = [
        jnp.dot(query_ref[t], cache_ref[t], preferred_element_type=F32) for t in range(requests)
    ]
    position = lax.broadcasted_iota(jnp.int32, scores[0].shape, 1)
    scores = [
        jnp.where(position < length_ref[t], scores[t] * scale, -jnp.inf) for t in range(requests)
    ]
    tops = [jnp.max(v, axis=1, keepdims=True) for v in scores]
    weights = [jnp.exp(v - top) for v, top in zip(scores, tops)]
    sums = [jnp.sum(v, axis=1, keepdims=True) for v in weights]
    probs = [(v / total).astype(BF16) for v, total in zip(weights, sums)]
    for t in range(requests):
        latent = lax.dot_general(
            probs[t], cache_ref[t, :LATENT], (((1,), (1,)), ((), ())), preferred_element_type=F32
        )
        latent = latent.astype(BF16).astype(F32)
        for c in range(LATENT // 128):
            latent_ref[c, t * heads : (t + 1) * heads, :] = latent[:, c * 128 : (c + 1) * 128]
    for copy in copies[1 + requests :]:
        copy.wait()
    for g in range(groups):
        for i in range(per):
            h = g * per + i
            latent = jnp.concatenate(
                [
                    latent_ref[c, pl.ds(h, requests, stride=heads), :]
                    for c in range(LATENT // 128)
                ],
                axis=1,
            ).astype(BF16)
            head = jnp.dot(latent, value_ref[g, i], preferred_element_type=F32)
            head_ref[:, h * VDIM : (h + 1) * VDIM] = head.astype(BF16)
    for out in outs:
        out[:, :wide] = head_ref[...]
    last.wait()


def attend(lengths, ids, residual, queries, cache, values, weight, roles):
    requests, heads, width = queries.shape
    groups = 4
    hbm = [
        pltpu.with_memory_space_constraint(w, pltpu.HBM)
        for w in (lengths, ids, queries, cache, values, weight)
    ]
    whole = pl.BlockSpec(memory_space=VMEM)
    return pl.pallas_call(
        attend_kernel,
        out_shape=(VMEM(weight.shape, weight.dtype),)
        + (jax.ShapeDtypeStruct((requests, heads * VDIM + 512), BF16),) * roles,
        in_specs=[whole] + [pl.BlockSpec(memory_space=pltpu.HBM)] * 6,
        out_specs=(whole,) * (1 + roles),
        scratch_shapes=[
            VMEM(queries.shape, BF16),
            VMEM(cache.shape, BF16),
            VMEM((groups, heads // groups) + values.shape[1:], BF16),
            VMEM((LATENT // 128, requests * heads, 128), F32),
            VMEM((requests, heads * VDIM), BF16),
            VMEM((2 * residual.shape[0], residual.shape[1] + 128), F32),
            pltpu.SMEM(lengths.shape, jnp.int32),
            pltpu.SMEM(ids.shape, jnp.int32),
            pltpu.SemaphoreType.DMA((requests,)),
            pltpu.SemaphoreType.DMA((groups,)),
            pltpu.SemaphoreType.DMA((4,)),
        ],
        compiler_params=pltpu.CompilerParams(vmem_limit_bytes=24 << 20),
        name="attend",
    )(residual, *hbm)


def combine_kernel(ids_ref, route_ref, received_ref, returned_ref, out_ref, sum_ref):
    roles, slots, _ = received_ref.shape
    share, width = out_ref.shape
    cols = width // roles
    for r in range(roles):
        kept = received_ref[r, :, cols:].astype(F32)
        for g in range(4):
            reach = min(256, cols - g * 256)
            start = r * cols + g * 256
            sum_ref[:, start : start + reach] = kept[g * share : (g + 1) * share, :reach]
    for t in range(share):
        extra = []
        for k in range(2):
            slot = slot_of(ids_ref, t, k)
            both = returned_ref[ids_ref[k, t]].astype(F32)
            one = jnp.where(slot % CAP == 0, both[0:1], both[1:2])
            extra.append(route_ref[k, t] * one)
        sum_ref[t : t + 1, :] += extra[0] + extra[1]
    out_ref[...] = sum_ref[...].astype(BF16)


def combine(ids, route, received, returned, share):
    width = returned.shape[2]
    whole = pl.BlockSpec(memory_space=VMEM)
    scalars = pl.BlockSpec(memory_space=pltpu.SMEM)
    return pl.pallas_call(
        combine_kernel,
        out_shape=jax.ShapeDtypeStruct((share, width), BF16),
        in_specs=[scalars] * 2 + [whole] * 2,
        out_specs=whole,
        scratch_shapes=[VMEM((share, width), F32)],
        compiler_params=pltpu.CompilerParams(vmem_limit_bytes=6 << 20),
        name="combine",
    )(ids, route, received, returned)


def load_kernel(gate_hbm, up_hbm, after_ref, both_ref, sems):
    half = both_ref.shape[2]
    parts = ((gate_hbm, 0), (gate_hbm, half), (up_hbm, 0))
    copies = [
        pltpu.make_async_copy(src.at[:, pl.ds(start, half)], both_ref.at[i], sems.at[i])
        for i, (src, start) in enumerate(parts)
    ]
    for copy in copies:
        copy.start()
    for copy in copies:
        copy.wait()


def load(gate, up, after):
    gate, up = [pltpu.with_memory_space_constraint(w, pltpu.HBM) for w in (gate, up)]
    return pl.pallas_call(
        load_kernel,
        out_shape=VMEM((3, gate.shape[0], gate.shape[1] // 2), gate.dtype),
        in_specs=[pl.BlockSpec(memory_space=pltpu.HBM)] * 2 + [pl.BlockSpec(memory_space=pl.ANY)],
        out_specs=pl.BlockSpec(memory_space=VMEM),
        scratch_shapes=[pltpu.SemaphoreType.DMA((3,))],
        compiler_params=pltpu.CompilerParams(vmem_limit_bytes=1 << 20),
        cost_estimate=pl.CostEstimate(
            flops=0, bytes_accessed=3 * gate.size, transcendentals=0
        ),
        name="load",
    )(gate, up, after)


def project_kernel(weight_ref, *refs):
    messages, out_ref = refs[:-1], refs[-1]
    depth = weight_ref.shape[0]
    rows = jnp.concatenate([m[:, :depth].astype(F32) for m in messages], axis=0).astype(BF16)
    out_ref[...] = jnp.dot(rows, weight_ref[...], preferred_element_type=F32)


def project(messages, weight):
    cols = weight.shape[1]
    tokens = sum(m.shape[0] for m in messages)
    whole = pl.BlockSpec(memory_space=VMEM)
    return pl.pallas_call(
        project_kernel,
        out_shape=jax.ShapeDtypeStruct((tokens, cols), F32),
        in_specs=[whole] * (1 + len(messages)),
        out_specs=whole,
        compiler_params=pltpu.CompilerParams(vmem_limit_bytes=6 << 20),
        name="project",
    )(pltpu.with_memory_space_constraint(weight, VMEM), *messages)


def dispatch_kernel(mine_ref, other_ref, *refs):
    messages, out_ref = refs[:-1], refs[-1]
    role, core = lax.axis_index("role"), lax.axis_index("head")
    roles = len(messages)
    tokens, cols = mine_ref.shape
    each = tokens // roles
    share = each // 2
    wide = messages[0].shape[1]
    left = 4 * 128
    slots = roles * CAP
    firsts, seconds = [], []
    for m in messages:
        side = m[:, wide - left :].astype(F32)
        turned = pltpu.roll(side, share, 0)
        firsts.append(jnp.where(core == 0, side, turned))
        seconds.append(jnp.where(core == 0, turned, side))
    second = jnp.concatenate(seconds, axis=0)
    resid = jnp.concatenate([jnp.concatenate(firsts, axis=0), second[:, : cols - left]], axis=1)
    notes = second[:, cols - left :].T
    attn_out = (mine_ref[...] + other_ref[...]).astype(BF16)
    hidden = (resid + attn_out.astype(F32)).astype(BF16)
    token = lax.broadcasted_iota(jnp.int32, (1, tokens), 1)
    source = role ^ (token // each)
    member = token % each
    row = lax.broadcasted_iota(jnp.int32, (roles * slots, 1), 0)
    dest, slot = row // slots, row % slots
    want = (dest * CAP + slot % CAP).astype(F32)
    placing = (
        (slot // CAP == source)
        & (member // share == core)
        & ((notes[0:1, :] == want) | (notes[1:2, :] == want))
    )
    keeping = (dest == source) & (member == core * share + slot % share)
    placed = jnp.dot(
        jnp.where(placing, 1.0, 0.0).astype(BF16), hidden, preferred_element_type=F32
    ).astype(BF16)
    kept = jnp.dot(jnp.where(keeping, 1.0, 0.0).astype(BF16), hidden, preferred_element_type=F32)
    kept = jnp.concatenate([kept, jnp.zeros((roles * slots, 1024 - cols), F32)], axis=1)
    group = slot // share
    extra = kept[:, :256]
    for g in range(1, 4):
        extra = jnp.where(group == g, kept[:, g * 256 : (g + 1) * 256], extra)
    extra = extra.astype(BF16)
    for d in range(roles):
        out_ref[d, :, :cols] = placed[d * slots : (d + 1) * slots]
        out_ref[d, :, cols:] = extra[d * slots : (d + 1) * slots]


def dispatch(mine, other, messages):
    roles = len(messages)
    cols = mine.shape[1]
    whole = pl.BlockSpec(memory_space=VMEM)
    return pl.pallas_call(
        dispatch_kernel,
        out_shape=jax.ShapeDtypeStruct((roles, roles * CAP, cols + 256), BF16),
        in_specs=[whole] * (2 + roles),
        out_specs=whole,
        compiler_params=pltpu.CompilerParams(vmem_limit_bytes=6 << 20),
        name="dispatch",
    )(mine, other, *messages)


def expert_kernel(
    mine_ref, other_ref, both_ref, up_hbm, down_hbm, keep_ref, send_ref,
    x_ref, act_ref, up_ref, down_ref, sems
):
    rows = mine_ref.shape[0]
    outs, _, broad = down_ref.shape
    half = both_ref.shape[2]

    def fetch(i):
        cols = pl.ds(i * broad, broad)
        return pltpu.make_async_copy(down_hbm.at[:, cols], down_ref.at[i], sems.at[i])

    rest = pltpu.make_async_copy(up_hbm.at[:, pl.ds(half, half)], up_ref, sems.at[outs])
    rest.start()
    fetch(0).start()
    x_ref[:rows, :] = mine_ref[...]
    x_ref[rows:, :] = other_ref[...]
    for i in range(2):
        gate = jnp.dot(x_ref[...], both_ref[i], preferred_element_type=F32)
        if i:
            for j in range(4, outs):
                fetch(j).start()
            rest.wait()
            up = jnp.dot(x_ref[...], up_ref[...], preferred_element_type=F32)
        else:
            up = jnp.dot(x_ref[...], both_ref[2], preferred_element_type=F32)
            for j in range(1, 4):
                fetch(j).start()
        act = (gate / (1.0 + jnp.exp(-gate)) * up).astype(BF16)
        act_ref[:, i * half : (i + 1) * half] = act
    for i in range(outs):
        fetch(i).wait()
        part = jnp.dot(act_ref[...], down_ref[i], preferred_element_type=F32)
        keep_ref[:, i * broad : (i + 1) * broad] = part[:rows]
        send_ref[:, i * broad : (i + 1) * broad] = part[rows:].astype(send_ref.dtype)


def run_experts(mine, other, both, up, down):
    rows, width = mine.shape
    units = up.shape[1]
    outs = 7
    both = pltpu.with_memory_space_constraint(both, VMEM)
    up, down = [pltpu.with_memory_space_constraint(w, pltpu.HBM) for w in (up, down)]
    whole = pl.BlockSpec(memory_space=VMEM)
    return pl.pallas_call(
        expert_kernel,
        out_shape=(
            jax.ShapeDtypeStruct((rows, width), F32),
            jax.ShapeDtypeStruct((rows, width), BF16),
        ),
        in_specs=[whole] * 3 + [pl.BlockSpec(memory_space=pltpu.HBM)] * 2,
        out_specs=(whole, whole),
        scratch_shapes=[
            VMEM((2 * rows, width), BF16),
            VMEM((2 * rows, units), BF16),
            VMEM((width, units // 2), BF16),
            VMEM((outs, units, width // outs), BF16),
            pltpu.SemaphoreType.DMA((outs + 1,)),
        ],
        compiler_params=pltpu.CompilerParams(vmem_limit_bytes=26 << 20),
        cost_estimate=pl.CostEstimate(
            flops=12 * rows * width * units, bytes_accessed=3 * width * units, transcendentals=0
        ),
        name="experts",
    )(mine, other, both, up, down)


def norm_kernel(received_ref, gain_ref, out_ref):
    roles = received_ref.shape[0]
    width = out_ref.shape[1]
    cols = width // roles
    total = jnp.float32(0.0)
    for r in range(roles):
        x = received_ref[r, :, :cols].astype(F32)
        total += jnp.sum(x * x, axis=1, keepdims=True)
    inverse = lax.rsqrt(total / width + 1e-06)
    for r in range(roles):
        x = received_ref[r, :, :cols].astype(F32)
        here = slice(r * cols, (r + 1) * cols)
        out_ref[:, here] = (x * inverse * gain_ref[:, here]).astype(BF16)


def normalise(received, gain):
    whole = pl.BlockSpec(memory_space=VMEM)
    return pl.pallas_call(
        norm_kernel,
        out_shape=jax.ShapeDtypeStruct((received.shape[1], gain.shape[1]), BF16),
        in_specs=[whole] * 2,
        out_specs=whole,
        compiler_params=pltpu.CompilerParams(vmem_limit_bytes=4 << 20),
        name="normalise",
    )(received, gain)


def fast(
    queries,
    kv_cache,
    cache_lengths,
    uv_weight,
    out_weight,
    residual,
    norm_gain,
    expert_ids,
    route_weights,
    gate_weight,
    up_weight,
    down_weight,
):
    roles = lax.axis_size("role")
    share = residual.shape[0]
    width = residual.shape[1]
    cols = width // roles
    ids = expert_ids.T
    cache = kv_cache.transpose(0, 2, 1)
    out_weight, *messages = attend(
        cache_lengths, ids, residual, queries, cache, uv_weight, out_weight, roles
    )
    both_weights = load(gate_weight, up_weight, messages[0])
    for step in sorted(range(1, roles), reverse=True):
        pairs = [(i, i ^ step) for i in range(roles)]
        messages[step] = lax.ppermute(messages[step], "role", pairs)
    messages, both_weights = lax.optimization_barrier((messages, both_weights))
    partial_value = project(messages, out_weight)
    other_value = lax.ppermute(partial_value, "head", [(0, 1), (1, 0)])
    outgoing = dispatch(partial_value, other_value, messages)
    received = lax.all_to_all(outgoing, "role", split_axis=0, concat_axis=0, tiled=True)
    normed = normalise(received, norm_gain.reshape(1, -1))
    other = lax.ppermute(normed, "head", [(0, 1), (1, 0)])
    keep, send = run_experts(normed, other, both_weights, up_weight, down_weight)
    sent = lax.ppermute(send, "head", [(0, 1), (1, 0)])
    summed = (keep + sent.astype(F32)).astype(BF16)
    returned = lax.all_to_all(
        summed.reshape(roles, CAP, width), "role", split_axis=0, concat_axis=0, tiled=True
    )
    return combine(ids, route_weights.T, received, returned, share)


def attend_general(queries, kv_cache, cache_lengths, uv_weight):
    scale_factor = (VDIM + ROPE) ** (-0.5)
    scores = (
        jnp.einsum("thc,tsc->ths", queries, kv_cache, preferred_element_type=jnp.float32)
        * scale_factor
    )
    position = lax.broadcasted_iota(jnp.int32, scores.shape, 2)
    scores = jnp.where(position < cache_lengths[:, None, None], scores, -jnp.inf)
    top_score = jnp.max(scores, axis=2, keepdims=True)
    weights = jnp.exp(scores - top_score)
    attn_probs = (weights / jnp.sum(weights, axis=2, keepdims=True)).astype(jnp.bfloat16)
    latent_out = jnp.einsum(
        "ths,tsc->thc", attn_probs, kv_cache[:, :, :LATENT], preferred_element_type=jnp.float32
    ).astype(jnp.bfloat16)
    head_out = jnp.einsum(
        "thc,hcv->thv", latent_out, uv_weight, preferred_element_type=jnp.float32
    ).astype(jnp.bfloat16)
    return head_out.reshape(head_out.shape[0], -1)


def general(
    queries,
    kv_cache,
    cache_lengths,
    uv_weight,
    out_weight,
    residual,
    norm_gain,
    expert_ids,
    route_weights,
    gate_weight,
    up_weight,
    down_weight,
):
    role_n = lax.axis_size("role")
    head_n = lax.axis_size("head")
    share_rows = residual.shape[0]
    model_width = residual.shape[1]
    head_out = attend_general(queries, kv_cache, cache_lengths, uv_weight)
    partial_value = jnp.dot(
        lax.all_gather(head_out, "role", axis=0, tiled=True),
        out_weight,
        preferred_element_type=jnp.float32,
    )
    summed_cols = lax.psum(partial_value, "head").astype(jnp.bfloat16)
    own_rows = lax.all_to_all(summed_cols, "role", split_axis=0, concat_axis=1, tiled=True)
    attn_out = lax.dynamic_slice_in_dim(
        own_rows, lax.axis_index("head") * share_rows, share_rows, 0
    )
    hidden = (residual.astype(jnp.float32) + attn_out.astype(jnp.float32)).astype(jnp.bfloat16)
    hidden_f = hidden.astype(jnp.float32)
    inverse = lax.rsqrt(jnp.mean(hidden_f * hidden_f, axis=1, keepdims=True) + 1e-06)
    normed = (hidden_f * inverse * norm_gain[None, :]).astype(jnp.bfloat16)
    flat_ids = expert_ids.reshape(-1)
    onehot = (
        flat_ids[:, None] == lax.broadcasted_iota(jnp.int32, (flat_ids.shape[0], EXPERTS), 1)
    ).astype(jnp.int32)
    slot_rank = jnp.sum(onehot * (jnp.cumsum(onehot, axis=0) - onehot), axis=1).reshape(
        expert_ids.shape
    )
    position = expert_ids * CAP + slot_rank
    slot_grid = lax.broadcasted_iota(jnp.int32, (EXPERTS * CAP,) + expert_ids.shape, 0)
    matches = slot_grid == position[None, :, :]
    placing = jnp.any(matches, axis=2).astype(jnp.bfloat16)
    mixing = jnp.sum(jnp.where(matches, route_weights[None, :, :], 0.0), axis=2).T
    buffer = (
        jnp.dot(placing, normed, preferred_element_type=jnp.float32)
        .astype(jnp.bfloat16)
        .reshape(EXPERTS, CAP, model_width)
    )
    devices = role_n * head_n
    group_size = devices // EXPERTS
    outgoing = jnp.repeat(buffer, group_size, axis=0)
    received = lax.all_to_all(outgoing, ("role", "head"), split_axis=0, concat_axis=0, tiled=True)
    item_count = received.shape[1]
    token_rows = received.reshape(-1, model_width)
    gate_val = jnp.dot(token_rows, gate_weight, preferred_element_type=jnp.float32)
    up_val = jnp.dot(token_rows, up_weight, preferred_element_type=jnp.float32)
    act_val = (jax.nn.silu(gate_val) * up_val).astype(jnp.bfloat16)
    expert_part = jnp.dot(act_val, down_weight, preferred_element_type=jnp.float32).reshape(
        devices, item_count, model_width
    )
    returned = lax.all_to_all(
        expert_part, ("role", "head"), split_axis=0, concat_axis=0, tiled=True
    )
    expert_out = jnp.sum(returned.reshape(EXPERTS, group_size, CAP, model_width), axis=1)
    combined = jnp.dot(
        mixing,
        expert_out.reshape(EXPERTS * CAP, model_width),
        precision=lax.Precision.HIGHEST,
        preferred_element_type=jnp.float32,
    )
    return (hidden_f + combined).astype(jnp.bfloat16)


def on_device(*arrays):
    residual = arrays[5]
    roles = lax.axis_size("role")
    fits = roles == EXPERTS and lax.axis_size("head") == 2 and residual.shape[0] == 4
    return (fast if fits and residual.shape[1] == roles * 896 else general)(*arrays)


def solution(mesh):
    return jax.shard_map(
        on_device,
        mesh=mesh,
        in_specs=(
            P(("groups", "role"), "head", None),
            P(("groups", "role"), None, None),
            P(("groups", "role")),
            P("head", None, None),
            P("head", "role"),
            P(("groups", "role", "head"), None),
            P(),
            P(("groups", "role", "head"), None),
            P(("groups", "role", "head"), None),
            P(None, ("role", "head")),
            P(None, ("role", "head")),
            P(("role", "head"), None),
        ),
        out_specs=P(("groups", "role", "head"), None),
        check_vma=False,
    )
```
